32 devices in a mesh: vec: 8 (over z, y), gz: 4 (over x, core).
Axes of the slice: x: 2, y: 2, z: 4, core: 2. Of those that a mesh axis runs over, the one named last changes fastest.
Arguments:
- base_flow: float32 [3, 128, 128, 128], P(None, 'gz'), may hold values from -6 to 6
- tangents: float32 [8, 3, 128, 128, 128], P('vec', None, 'gz'), may hold values from -6 to 6
- shells: int32 [4], replicated, may hold values from 1 to 31
Outputs:
- base_next: float32 [3, 128, 128, 128], P(None, 'gz', 'vec')
- ortho_tangents: float32 [8, 3, 128, 128, 128], P('vec', None, 'gz')
- growth: float32 [8], replicated
The draws below stay inside these ranges and needn't reach their ends.
Inputs may be any that keep to these rules, and one draw needn't show every extreme that they name: `shells`: repeats may occur.
All inputs are finite; a program needn't handle non-finite values.
Results may differ from the reference program's by a relative error of at most 0.00017.
Values sent between devices are 32-bit elements; how exact they have to be, the bound alone decides.
No kernel may reach another device: no remote copies, remote signals or barrier semaphores. Data moves between devices by JAX's collectives and lax.ppermute only.
A program may use at most 256 MiB of HBM per device.

```python
import math
import jax
import jax.numpy as jnp
from jax import lax

NX = 128
NY = 128
NZ = 128
NFORCE = 4
VECS = 8


def set_ends(array, own_key, least, largest):
    longest = array.shape.index(max(array.shape))
    spots = []
    for shift in (0, 1):
        where = [jax.random.randint(jax.random.fold_in(own_key, axis), (), 0, length) for axis, length in enumerate(array.shape)]
        where[longest] = (where[longest] + shift) % array.shape[longest]
        spots.append(tuple(where))
    return array.at[spots[0]].set(least).at[spots[1]].set(largest)


def steps_of(key, shape, split, smallest, top_value):
    factor_of, own = 1.0, jax.random.fold_in(key, 6)
    for dim, blocks in split:
        draws = jnp.exp(jax.random.uniform(jax.random.fold_in(own, dim), (blocks,), jnp.float32, smallest / len(split), top_value / len(split)))
        factor_of = factor_of * jnp.repeat(draws, shape[dim] // blocks).reshape([-1 if axis == dim else 1 for axis in range(len(shape))])
    return factor_of


def bell_draw(key, shape, width, reach, cuts=(), held_as=jnp.bfloat16):
    entries = jax.random.normal(key, shape, jnp.float32) * width
    if len(cuts) > 0:
        entries = steps_of(key, shape, cuts, -0.22, 0.18) * entries
    return jnp.clip(entries, min=-reach, max=reach).astype(held_as)


def setup_inputs(seed: int = 0) -> dict:
    key_list = jax.random.split(jax.random.key(seed), 4)
    return {
        "base_flow": bell_draw(key_list[0], (3, NZ, NY, NX), 1.0, 6.0, ((1, 4),), jnp.float32),
        "tangents": bell_draw(key_list[1], (VECS, 3, NZ, NY, NX), 1.0, 6.0, ((0, 8), (2, 4)), jnp.float32),
        "shells": set_ends(jax.random.randint(key_list[2], (NFORCE,), 1, NZ // 4), jax.random.fold_in(key_list[2], 1), 1, (NZ // 4) - 1).astype(jnp.int32),
    }


time_step = 0.005
viscosity = 0.01
forcing_amplitude = 4.0
highest = lax.Precision.HIGHEST

def grid_spacing():
    return 2.0 * math.pi / NX

def central(field, axis):
    return (jnp.roll(field, -1, axis) - jnp.roll(field, 1, axis)) / (2.0 * grid_spacing())

def laplacian(field):
    spacing = grid_spacing()
    summed = -6.0 * field
    for axis in (-1, -2, -3):
        summed = summed + jnp.roll(field, -1, axis) + jnp.roll(field, 1, axis)
    return summed / (spacing * spacing)

def forcing_field(shells):
    positions = jnp.arange(NZ, dtype=jnp.int32)
    angles = 2.0 * math.pi / NZ * (shells[:, None] * positions[None, :] % NZ).astype(jnp.float32)
    profile = forcing_amplitude * jnp.sum(jnp.sin(angles), axis=0)
    first = jnp.broadcast_to(profile[:, None, None], (NZ, NY, NX))
    zeros = jnp.zeros((NZ, NY, NX), jnp.float32)
    return jnp.stack([first, zeros, zeros])

def wave_symbols():
    spacing = grid_spacing()
    wave_z = jnp.arange(NZ, dtype=jnp.int32)[:, None, None]
    wave_y = jnp.arange(NY, dtype=jnp.int32)[None, :, None]
    wave_x = jnp.arange(NX, dtype=jnp.int32)[None, None, :]

    def slope(wave, length):
        return jnp.sin(2.0 * math.pi / length * wave.astype(jnp.float32)) / spacing
    shape = (NZ, NY, NX)
    vectors = jnp.stack([jnp.broadcast_to(slope(wave_x, NX), shape), jnp.broadcast_to(slope(wave_y, NY), shape), jnp.broadcast_to(slope(wave_z, NZ), shape)])
    resting = (wave_x % (NX // 2) == 0) & (wave_y % (NY // 2) == 0) & (wave_z % (NZ // 2) == 0)
    squared = jnp.sum(vectors * vectors, axis=0)
    inverse = jnp.where(resting, 0.0, 1.0 / jnp.where(resting, 1.0, squared))
    return (vectors, inverse)

def project(rates):
    vectors, inverse = wave_symbols()
    spectrum = jnp.fft.fftn(rates, axes=(1, 2, 3))
    normal_part = jnp.sum(vectors * spectrum, axis=0, keepdims=True)
    return jnp.real(jnp.fft.ifftn(spectrum - vectors * normal_part * inverse, axes=(1, 2, 3))).astype(jnp.float32)

def base_rate(velocity, forcing):
    advect = velocity[0][None] * central(velocity, -1)
    advect = advect + velocity[1][None] * central(velocity, -2)
    advect = advect + velocity[2][None] * central(velocity, -3)
    return -advect + viscosity * laplacian(velocity) + forcing

def tangent_rate(tangent, velocity):
    advect = jnp.zeros_like(tangent)
    for direction in range(3):
        axis = -1 - direction
        advect = advect + velocity[direction][None] * central(tangent, axis)
        advect = advect + tangent[direction][None] * central(velocity, axis)
    return -advect + viscosity * laplacian(tangent)

def reference(base_flow, tangents, shells):
    forcing = forcing_field(shells)
    base_next = base_flow + time_step * project(base_rate(base_flow, forcing))

    def advance_one(tangent):
        return tangent + time_step * project(tangent_rate(tangent, base_flow))
    advanced = lax.map(advance_one, tangents)
    flattened = advanced.reshape(advanced.shape[0], -1)
    gram_matrix = jnp.dot(flattened, flattened.T, precision=highest) / flattened.shape[1]
    factor = jnp.linalg.cholesky(gram_matrix)
    ortho_rows = lax.linalg.triangular_solve(factor, flattened, left_side=True, lower=True)
    return (base_next, ortho_rows.reshape(tangents.shape), jnp.log(jnp.diagonal(factor)))
```

```python
import functools
import math

import jax
import jax.numpy as jnp
import ml_dtypes
import numpy as np
from jax import lax
from jax.experimental import pallas as pl
from jax.experimental.pallas import tpu as pltpu
from jax.sharding import PartitionSpec as P

time_step = 0.005
viscosity = 0.01
forcing_amplitude = 4.0

TILE = 16
PAD = 8
VMEM_BYTES = 52 * 1024 * 1024


def spacing_of(nx):
    return 2.0 * math.pi / nx


def real_basis(length):
    cells = np.arange(length)
    columns = [np.full(length, 1.0 / np.sqrt(length)), (-1.0) ** cells / np.sqrt(length)]
    waves = [0, length // 2]
    for wave in range(1, length // 2):
        angle = 2.0 * np.pi * ((cells * wave) % length) / length
        columns += [np.sqrt(2.0 / length) * np.cos(angle), np.sqrt(2.0 / length) * np.sin(angle)]
        waves += [wave, wave]
    sines = np.sin(2.0 * np.pi * np.array(waves) / length) ** 2
    sines[:2] = 0.0
    return np.stack(columns, axis=1), sines


def halves(matrix):
    high = matrix.astype(np.float32).astype(ml_dtypes.bfloat16)
    low = (matrix - high.astype(np.float64)).astype(np.float32).astype(ml_dtypes.bfloat16)
    return high, low


def right_table(matrix):
    high, low = halves(matrix)
    return np.concatenate(
        [np.concatenate([high, low], axis=1), np.concatenate([high, low], axis=1)], axis=0
    )


def left_table(matrix):
    high, low = halves(matrix)
    return np.concatenate(
        [np.concatenate([high, high], axis=1), np.concatenate([low, low], axis=1)], axis=0
    )


def column_tables(sines_y, sines_x):
    four = 4.0 * (sines_y[:, None] + sines_x[None, :])
    resting = four == 0.0
    decay = 1.0 / (1.0 + four / 2.0 + np.sqrt(four + four * four / 4.0))
    green = np.where(resting, 0.0, -decay / np.where(resting, 1.0, 1.0 - decay * decay))
    return decay, green, resting


def split_cat(data, axis):
    high = data.astype(jnp.bfloat16)
    low = (data - high.astype(jnp.float32)).astype(jnp.bfloat16)
    return jnp.concatenate([high, low], axis=axis)


def right_product(data, table):
    out = jnp.dot(split_cat(data, 1), table, preferred_element_type=jnp.float32)
    width = out.shape[1] // 2
    return out[:, :width] + out[:, width:]


def left_product(table, data):
    out = jnp.dot(table, split_cat(data, 0), preferred_element_type=jnp.float32)
    height = out.shape[0] // 2
    return out[:height] + out[height:]


def rate_kernel(tangent, chunk, layers, *refs):
    if tangent:
        (place, u_hbm, v_hbm, lo_hbm, hi_hbm, decay, mark, qx, qy) = refs[:9]
        (a_out, f_out, m_out, us, vs, rz, ry, dv, pw, sems, halo_sems) = refs[9:]
    else:
        (place, profile, v_hbm, lo_hbm, hi_hbm, decay, mark, qx, qy) = refs[:9]
        (a_out, f_out, m_out, vs, rz, ry, dv, pw, sems, halo_sems) = refs[9:]
        us = vs
    step = pl.program_id(0)
    steps = layers // chunk
    ny, nx = f_out.shape[1], f_out.shape[2]
    space = spacing_of(nx)
    adv_scale = -time_step / (2.0 * space)
    lap_scale = viscosity * time_step / (space * space)
    fields = [(v_hbm, vs)]
    if tangent:
        fields.append((u_hbm, us))
    inner = pl.ds(PAD, ny)

    def chunk_copies(k):
        return [
            pltpu.make_async_copy(
                source.at[:, pl.ds(k * chunk, chunk)],
                target.at[:, pl.ds(k * chunk + 2, chunk), inner],
                sems.at[k, i],
            )
            for i, (source, target) in enumerate(fields)
        ]

    def halo_copies(side):
        source = (lo_hbm, hi_hbm)[side]
        near, far = ((1, 0), (layers + 2, layers + 3))[side]
        out = [
            pltpu.make_async_copy(
                source.at[pl.ds(0, 3)], vs.at[:, near, inner], halo_sems.at[side, 0]
            ),
            pltpu.make_async_copy(source.at[6], vs.at[2, far, inner], halo_sems.at[side, 1]),
        ]
        if tangent:
            out += [
                pltpu.make_async_copy(
                    source.at[pl.ds(3, 3)], us.at[:, near, inner], halo_sems.at[side, 2]
                ),
                pltpu.make_async_copy(source.at[7], us.at[2, far, inner], halo_sems.at[side, 3]),
            ]
        return out

    def wrap_rows(ref, index):
        ref[index + (pl.ds(0, PAD),)] = ref[index + (pl.ds(ny, PAD),)]
        ref[index + (pl.ds(ny + PAD, PAD),)] = ref[index + (pl.ds(PAD, PAD),)]

    def wrap_layers(first, count):
        def body(i, carry):
            for _, ref in fields:
                for c in range(3):
                    wrap_rows(ref, (c, first + i))
            return carry

        lax.fori_loop(0, count, body, 0)

    def wait_chunk(k):
        for copy in chunk_copies(k):
            copy.wait()
        wrap_layers(k * chunk + 2, chunk)

    def wait_halo(side):
        for copy in halo_copies(side):
            copy.wait()
        near, far = ((1, 0), (layers + 2, layers + 3))[side]
        wrap_layers(near, 1)
        for _, ref in fields:
            wrap_rows(ref, (2, far))

    def rate_tile(layer, y0, comps):
        rows = pl.ds(PAD + y0, TILE)
        flow = [vs[c, layer, rows] for c in range(3)]
        drift = [us[c, layer, rows] for c in range(3)] if tangent else flow
        out = []

        def neighbours(ref, c, centre):
            return (
                pltpu.roll(centre, nx - 1, 1),
                pltpu.roll(centre, 1, 1),
                ref[c, layer, pl.ds(PAD + y0 + 1, TILE)],
                ref[c, layer, pl.ds(PAD + y0 - 1, TILE)],
                ref[c, layer + 1, rows],
                ref[c, layer - 1, rows],
            )

        for c in comps:
            xp, xm, yp, ym, zp, zm = neighbours(us, c, drift[c])
            adv = flow[0] * (xp - xm) + flow[1] * (yp - ym) + flow[2] * (zp - zm)
            lap = ((xp + xm) + (yp + ym)) + ((zp + zm) - 6.0 * drift[c])
            if tangent:
                xp, xm, yp, ym, zp, zm = neighbours(vs, c, flow[c])
                adv = adv + (
                    drift[0] * (xp - xm) + drift[1] * (yp - ym) + drift[2] * (zp - zm)
                )
            out.append(adv_scale * adv + lap_scale * lap)
        return drift, out

    def z_rate(layer, slot):
        for y0 in range(0, ny, TILE):
            _, (rate,) = rate_tile(layer, y0, (2,))
            rz[slot, pl.ds(y0, TILE)] = rate

    @pl.when(step == 0)
    def _():
        for copy in halo_copies(0):
            copy.start()
        for k in range(steps):
            for copy in chunk_copies(k):
                copy.start()
        for copy in halo_copies(1):
            copy.start()
        wait_halo(0)
        wait_chunk(0)
        if steps == 1:
            wait_halo(1)
        z_rate(1, 0)
        z_rate(2, 1)
        m_out[...] = jnp.zeros(m_out.shape, jnp.float32)
        start = (place[0] * (layers // 2)).astype(jnp.float32)
        pw[...] = jnp.where(mark[...] > 0.0, start, 1.0)

    @pl.when(step + 1 < steps)
    def _():
        wait_chunk(step + 1)

    if steps > 1:

        @pl.when(step + 1 == steps)
        def _():
            wait_halo(1)

    def layer_body(i, carry):
        layer = step * chunk + i + 2
        for y0 in range(0, ny, TILE):
            rows = pl.ds(y0, TILE)
            drift, (rate_x, rate_y) = rate_tile(layer, y0, (0, 1))
            if not tangent:
                rate_x = rate_x + profile[step * chunk + i]
            a_out[0, i, rows] = drift[0] + rate_x
            a_out[1, i, rows] = drift[1] + rate_y
            a_out[2, i, rows] = drift[2] + rz[1, rows]
            dv[i, rows] = pltpu.roll(rate_x, nx - 1, 1) - pltpu.roll(rate_x, 1, 1)
            ry[pl.ds(PAD + y0, TILE)] = rate_y
        z_rate(layer + 1, 2)
        wrap_rows(ry, ())
        for y0 in range(0, ny, TILE):
            rows = pl.ds(y0, TILE)
            along_y = ry[pl.ds(PAD + y0 + 1, TILE)] - ry[pl.ds(PAD + y0 - 1, TILE)]
            middle, upper = rz[1, rows], rz[2, rows]
            along_z = upper - rz[0, rows]
            dv[i, rows] = dv[i, rows] + (along_y + along_z)
            rz[0, rows] = middle
            rz[1, rows] = upper
        return carry

    lax.fori_loop(0, chunk, layer_body, 0)

    waves = right_product(dv[...].reshape(chunk * ny, nx), qx[...]).reshape(chunk, ny, nx)
    waves = left_product(qy[...], jnp.concatenate([waves[i] for i in range(chunk)], axis=1))
    for i in range(chunk):
        f_out[i] = waves[:, i * nx : (i + 1) * nx]
    for y0 in range(0, ny, TILE):
        rows = pl.ds(y0, TILE)
        rate = decay[rows]
        marks = mark[rows]
        power = pw[rows]
        right = [m_out[0, rows], m_out[1, rows]]
        left = [m_out[2, rows], m_out[3, rows]]
        for i in range(chunk):
            f = f_out[i, rows]
            parity = i % 2
            right[parity] = rate * right[parity] + f
            left[parity] = left[parity] + power * f
            if parity == 1:
                power = rate * power + marks
        pw[rows] = power
        m_out[0, rows], m_out[1, rows] = right
        m_out[2, rows], m_out[3, rows] = left


def solve_kernel(chunk, layers, period, rows_out, *refs):
    (place, f_in, sides, totals, wrap_l, wrap_r, decay, green, mark, qy, qx, a_in) = refs[:12]
    (v_out, qm, hat, phi) = refs[12:]
    step = pl.program_id(0)
    ny, nx = f_in.shape[1], f_in.shape[2]
    tall = rows_out + 2 * PAD
    half = layers // 2

    def sweep(y0, resting):
        size = PAD if resting else TILE
        rows = pl.ds(y0, size)
        rate = decay[rows]
        factor = green[rows]
        left = [sides[p, rows] + wrap_l[rows] * totals[p, rows] for p in range(2)]
        right = [sides[2 + p, rows] + wrap_r[rows] * totals[2 + p, rows] for p in range(2)]
        back = list(right)
        for z in reversed(range(layers)):
            f = f_in[z, rows]
            part = rate * back[z % 2]
            qm[z, rows] = part
            back[z % 2] = part + f
        hat[0, rows] = factor * (left[1] + rate * back[1])
        ahead = list(left)
        for z in range(layers):
            ahead[z % 2] = rate * ahead[z % 2] + f_in[z, rows]
            hat[z + 1, rows] = factor * (ahead[z % 2] + qm[z, rows])
        hat[layers + 1, rows] = factor * (rate * ahead[0] + right[0])

    def resting_columns():
        rows = pl.ds(0, PAD)
        marked = mark[rows] > 0.0
        start = place[0] * half
        for p in range(2):
            own0 = jnp.zeros((PAD, nx), jnp.float32)
            own1 = jnp.zeros((PAD, nx), jnp.float32)
            for j in range(half):
                f = f_in[2 * j + p, rows]
                own0 = own0 + f
                own1 = own1 + (start + j).astype(jnp.float32) * f
            left0 = sides[p, rows]
            right1 = sides[2 + p, rows]
            all0 = totals[p, rows]
            all1 = totals[2 + p, rows]
            right0 = all0 - own0 - left0
            left1 = all1 - own1 - right1
            prefix = jnp.zeros((PAD, nx), jnp.float32)
            twice = jnp.zeros((PAD, nx), jnp.float32)
            first, last = (0, half + 1) if p == 0 else (-1, half)
            for j in range(first, last):
                t = (start + j).astype(jnp.float32)
                if j > 0:
                    twice = twice + prefix
                if 0 <= j < half:
                    prefix = prefix + f_in[2 * j + p, rows]
                value = 0.5 * (t * (left0 - right0 - own0) + (right1 - left1 + own1)) + twice
                value = value - t * (t * all0 - 2.0 * all1) * (0.5 / period)
                z = 2 * j + p + 1
                hat[z, rows] = jnp.where(marked, value, hat[z, rows])

    def invert(first, count, slot):
        cols = jnp.concatenate([hat[first + i] for i in range(count)], axis=1)
        out = left_product(qy[...], cols)
        out = jnp.concatenate([out[:, i * nx : (i + 1) * nx] for i in range(count)], axis=0)
        out = right_product(out, qx[...])
        for i in range(count):
            phi[slot + i] = out[i * tall : (i + 1) * tall]

    @pl.when(step == 0)
    def _():
        def body(i, carry):
            sweep(pl.multiple_of(i * TILE, TILE), False)
            return carry

        lax.fori_loop(0, ny // TILE, body, 0)
        resting_columns()
        invert(0, 2, 0)

    invert(step * chunk + 2, chunk, 2)

    for i in range(chunk):
        for y0 in range(0, rows_out, TILE):
            rows = pl.ds(y0, TILE)
            layer = i + 1
            here = phi[layer, pl.ds(PAD + y0, TILE)]
            v_out[0, i, rows] = a_in[0, i, rows] - (
                pltpu.roll(here, nx - 1, 1) - pltpu.roll(here, 1, 1)
            )
            v_out[1, i, rows] = a_in[1, i, rows] - (
                phi[layer, pl.ds(PAD + y0 + 1, TILE)] - phi[layer, pl.ds(PAD + y0 - 1, TILE)]
            )
            v_out[2, i, rows] = a_in[2, i, rows] - (
                phi[layer + 1, pl.ds(PAD + y0, TILE)] - phi[layer - 1, pl.ds(PAD + y0, TILE)]
            )
    for i in range(2):
        phi[i] = phi[chunk + i]


def pairs_of(count):
    return [(i, j) for i in range(count) for j in range(i + 1)]


def gram_kernel(count, x_ref, out_ref, acc):
    step = pl.program_id(0)
    rows = x_ref.shape[1]

    @pl.when(step == 0)
    def _():
        acc[...] = jnp.zeros(acc.shape, jnp.float32)

    group = 8
    for bi in range(0, count, group):
        for bj in range(0, bi + 1, group):
            pairs = [
                (i, j)
                for i in range(bi, min(bi + group, count))
                for j in range(bj, min(bj + group, count))
                if j <= i
            ]
            slots = [i * (i + 1) // 2 + j for i, j in pairs]

            def body(t, sums):
                part = pl.ds(pl.multiple_of(t * 8, 8), 8)
                needed = sorted({i for i, _ in pairs} | {j for _, j in pairs})
                tile = {i: x_ref[i, part] for i in needed}
                return tuple(s + tile[i] * tile[j] for s, (i, j) in zip(sums, pairs))

            sums = lax.fori_loop(0, rows // 8, body, tuple(acc[s] for s in slots))
            for s, value in zip(slots, sums):
                acc[s] = value

    @pl.when(step == pl.num_programs(0) - 1)
    def _():
        shape = out_ref.shape
        row = lax.broadcasted_iota(jnp.int32, shape, 0)
        lane = lax.broadcasted_iota(jnp.int32, shape, 1)
        out = jnp.zeros(shape, jnp.float32)
        for s, (i, j) in enumerate(pairs_of(count)):
            total = jnp.sum(jnp.sum(acc[s], axis=0, keepdims=True), axis=1, keepdims=True)
            hit = ((row == i) & (lane == j)) | ((row == j) & (lane == i))
            out = jnp.where(hit, total, out)
        out_ref[...] = out


def ortho_kernel(count, cells, parts_ref, x_ref, out_ref, growth_ref, coef):
    step = pl.program_id(0)
    rows = x_ref.shape[1]

    @pl.when(step == 0)
    def _():
        shape = parts_ref.shape[1:]
        row = lax.broadcasted_iota(jnp.int32, shape, 0)
        lane = lax.broadcasted_iota(jnp.int32, shape, 1)
        work = jnp.sum(parts_ref[...], axis=0) / cells
        work = jnp.where(lane == row + count, 1.0, work)
        for k in range(count - 1):
            pivot = work[k : k + 1, k : k + 1]
            scale = jnp.where(row[:, :1] > k, work[:, k : k + 1] / pivot, 0.0)
            work = work - scale * work[k : k + 1, :]
        diagonal = jnp.sum(jnp.where(lane == row, work, 0.0), axis=1, keepdims=True)
        growth_ref[...] = jnp.broadcast_to(0.5 * jnp.log(diagonal), shape)
        work = work / jnp.sqrt(diagonal)
        for s, (i, j) in enumerate(pairs_of(count)):
            coef[s] = jnp.broadcast_to(
                work[i : i + 1, count + j : count + j + 1], coef.shape[1:]
            )

    def body(t, carry):
        part = pl.ds(pl.multiple_of(t * 16, 16), 16)
        tile = [x_ref[i, part] for i in range(count)]
        for i in range(count):
            total = None
            for j in range(i + 1):
                c = coef[i * (i + 1) // 2 + j]
                term = jnp.concatenate([c, c], axis=0) * tile[j]
                total = term if total is None else total + term
            out_ref[i, part] = total
        return carry

    lax.fori_loop(0, rows // 16, body, 0)


def params(limit=VMEM_BYTES):
    return pltpu.CompilerParams(vmem_limit_bytes=limit)


def whole(shape):
    return pl.BlockSpec(shape, lambda *_: (0,) * len(shape))


ANY = pl.BlockSpec(memory_space=pl.ANY)
SMEM = pl.BlockSpec(memory_space=pltpu.SMEM)


def rates(place, extra, velocity, lo, hi, tables):
    _, layers, ny, nx = velocity.shape
    tangent = extra.ndim == 4
    chunk = 4 if layers % 4 == 0 else 2
    field = pltpu.VMEM((3, layers + 4, ny + 2 * PAD, nx), jnp.float32)
    scratch = [field, field] if tangent else [field]
    scratch += [
        pltpu.VMEM((3, ny, nx), jnp.float32),
        pltpu.VMEM((ny + 2 * PAD, nx), jnp.float32),
        pltpu.VMEM((chunk, ny, nx), jnp.float32),
        pltpu.VMEM((ny, nx), jnp.float32),
        pltpu.SemaphoreType.DMA((layers // chunk, 2)),
        pltpu.SemaphoreType.DMA((2, 4)),
    ]
    size = velocity.size
    return pl.pallas_call(
        functools.partial(rate_kernel, tangent, chunk, layers),
        grid=(layers // chunk,),
        in_specs=[SMEM, ANY if tangent else SMEM, ANY, ANY, ANY]
        + [whole(t.shape) for t in tables],
        out_specs=[
            pl.BlockSpec((3, chunk, ny, nx), lambda g: (0, g, 0, 0)),
            pl.BlockSpec((chunk, ny, nx), lambda g: (g, 0, 0)),
            whole((4, ny, nx)),
        ],
        out_shape=[
            jax.ShapeDtypeStruct(velocity.shape, jnp.float32),
            jax.ShapeDtypeStruct((layers, ny, nx), jnp.float32),
            jax.ShapeDtypeStruct((4, ny, nx), jnp.float32),
        ],
        scratch_shapes=scratch,
        compiler_params=params(),
        cost_estimate=pl.CostEstimate(
            flops=60 * size, bytes_accessed=16 * size, transcendentals=0
        ),
        name="tangent_rates" if tangent else "base_rates",
    )(place, extra, velocity, lo, hi, *tables)


def solve(place, f, sides, totals, wraps, tables, a, rows_out, period, block):
    layers, ny, nx = f.shape
    chunk = 4 if layers % 4 == 0 else 2
    tall = rows_out + 2 * PAD
    moments = whole((4, ny, nx))
    return pl.pallas_call(
        functools.partial(solve_kernel, chunk, layers, period, rows_out),
        grid_spec=pltpu.PrefetchScalarGridSpec(
            num_scalar_prefetch=1,
            grid=(layers // chunk,),
            in_specs=[whole(f.shape), moments, moments, whole((ny, nx)), whole((ny, nx))]
            + [whole(t.shape) for t in tables]
            + [pl.BlockSpec((3, chunk, rows_out, nx), lambda g, p: (0, g, p[1] * block, 0))],
            out_specs=pl.BlockSpec((3, chunk, rows_out, nx), lambda g, p: (0, g, 0, 0)),
            scratch_shapes=[
                pltpu.VMEM((layers, ny, nx), jnp.float32),
                pltpu.VMEM((layers + 2, ny, nx), jnp.float32),
                pltpu.VMEM((chunk + 2, tall, nx), jnp.float32),
            ],
        ),
        out_shape=jax.ShapeDtypeStruct((3, layers, rows_out, nx), jnp.float32),
        compiler_params=params(),
        cost_estimate=pl.CostEstimate(
            flops=40 * a.size, bytes_accessed=12 * a.size, transcendentals=0
        ),
        name="tangent_solve" if rows_out == ny else "base_solve",
    )(place, f, sides, totals, *wraps, *tables, a)


def row_chunk(rows):
    best = 16
    for size in range(16, 200, 16):
        if rows % size == 0:
            best = size
    return best


def gram(cells):
    count, rows, nx = cells.shape
    size = row_chunk(rows)
    tall = max(8, count)
    return pl.pallas_call(
        functools.partial(gram_kernel, count),
        grid=(rows // size,),
        in_specs=[pl.BlockSpec((count, size, nx), lambda g: (0, g, 0))],
        out_specs=whole((tall, nx)),
        out_shape=jax.ShapeDtypeStruct((tall, nx), jnp.float32),
        scratch_shapes=[pltpu.VMEM((count * (count + 1) // 2, 8, nx), jnp.float32)],
        compiler_params=params(),
        cost_estimate=pl.CostEstimate(
            flops=count * cells.size, bytes_accessed=4 * cells.size, transcendentals=0
        ),
        name="gram_parts",
    )(cells)


def ortho(parts, cells, total_cells):
    count, rows, nx = cells.shape
    size = row_chunk(rows)
    return pl.pallas_call(
        functools.partial(ortho_kernel, count, total_cells),
        grid=(rows // size,),
        in_specs=[whole(parts.shape), pl.BlockSpec((count, size, nx), lambda g: (0, g, 0))],
        out_specs=[
            pl.BlockSpec((count, size, nx), lambda g: (0, g, 0)),
            whole(parts.shape[1:]),
        ],
        out_shape=[
            jax.ShapeDtypeStruct(cells.shape, jnp.float32),
            jax.ShapeDtypeStruct(parts.shape[1:], jnp.float32),
        ],
        scratch_shapes=[pltpu.VMEM((count * (count + 1) // 2, 8, nx), jnp.float32)],
        compiler_params=params(),
        cost_estimate=pl.CostEstimate(
            flops=count * cells.size, bytes_accessed=8 * cells.size, transcendentals=0
        ),
        name="ortho_rows",
    )(parts, cells)


def ring_shift(block, shift):
    count = lax.axis_size("gz")
    return lax.ppermute(block, "gz", [(i, (i + shift) % count) for i in range(count)])


def side_sums(moments, slab_power):
    count = lax.axis_size("gz")
    here = lax.axis_index("gz")
    right, left = moments[:2], moments[2:]
    from_left = jnp.zeros_like(right)
    from_right = jnp.zeros_like(left)
    span = 1
    while span < count:
        swapped = lax.ppermute(
            jnp.concatenate([right, left], axis=0), "gz", [(i, i ^ span) for i in range(count)]
        )
        other_right, other_left = swapped[:2], swapped[2:]
        inside = here % span
        upper = (here // span) % 2 == 1
        to_left = slab_power(inside)
        to_right = slab_power(span - 1 - inside)
        from_left = jnp.where(upper, from_left + to_left * other_right, from_left)
        from_right = jnp.where(upper, from_right, from_right + to_right * other_left)
        across = slab_power(span)
        right = jnp.where(upper, right + across * other_right, other_right + across * right)
        left = jnp.where(upper, other_left + across * left, left + across * other_left)
        span *= 2
    return jnp.concatenate([from_left, from_right], axis=0), jnp.concatenate([right, left], axis=0)


def per_device(base_flow, tangents, shells):
    _, layers, ny, nx = base_flow.shape
    slabs = lax.axis_size("gz")
    vectors = lax.axis_size("vec")
    here = lax.axis_index("gz")
    mine = lax.axis_index("vec")
    nz = slabs * layers
    period = nz // 2
    tangent = tangents[0]

    basis_x, sines_x = real_basis(nx)
    basis_y, sines_y = real_basis(ny)
    decay64, green64, resting = column_tables(sines_y, sines_x)
    decay = jnp.asarray(decay64, jnp.float32)
    green = jnp.asarray(green64, jnp.float32)
    mark = jnp.asarray(resting, jnp.float32)
    slab_log = jnp.asarray((layers // 2) * np.log(decay64), jnp.float32)
    closing = jnp.asarray(
        np.where(resting, 0.0, 1.0 / np.where(resting, 1.0, 1.0 - decay64**period)), jnp.float32
    )

    def slab_power(exponent):
        return jnp.exp(jnp.asarray(exponent).astype(jnp.float32) * slab_log)

    wraps = (closing * slab_power(here), closing * slab_power(slabs - 1 - here))
    qx_forward = jnp.asarray(right_table(basis_x))
    qy_forward = jnp.asarray(left_table(basis_y.T))
    qx_inverse = jnp.asarray(right_table(basis_x.T))
    rows_out = ny // vectors

    def rows_table(first, count):
        high, low = halves(np.concatenate([basis_y, basis_y, basis_y], axis=0))
        both = []
        for part in (high, low):
            part = lax.dynamic_slice_in_dim(jnp.asarray(part), ny + first - PAD, count + 2 * PAD, 0)
            both.append(jnp.concatenate([part, part], axis=1))
        return jnp.concatenate(both, axis=0)

    def edge(near, far):
        return jnp.concatenate(
            [base_flow[:, near], tangent[:, near], base_flow[2:, far], tangent[2:, far]], axis=0
        )

    lo = ring_shift(edge(layers - 1, layers - 2), 1)
    hi = ring_shift(edge(0, 1), -1)

    rows_run = max(rows_out, TILE)
    block = mine * rows_out // rows_run
    place = jnp.stack([here, block]).astype(jnp.int32)
    rate_tables = (decay, mark, qx_forward, qy_forward)
    a, f, moments = rates(place, tangent, base_flow, lo, hi, rate_tables)
    sides, totals = side_sums(moments, slab_power)
    tables = (decay, green, mark, rows_table(0, ny), qx_inverse)
    advanced = solve(place, f, sides, totals, wraps, tables, a, ny, period, 0)

    piece_rows = 3 * layers * ny // vectors
    cells = lax.all_to_all(
        advanced.reshape(vectors, piece_rows, nx), "vec", split_axis=0, concat_axis=0, tiled=True
    )

    positions = (here * layers + jnp.arange(layers, dtype=jnp.int32)) % nz
    angles = 2.0 * math.pi / nz * (shells[:, None] * positions[None, :] % nz).astype(jnp.float32)
    profile = time_step * forcing_amplitude * jnp.sum(jnp.sin(angles), axis=0)
    base_a, base_f, base_moments = rates(place, profile, base_flow, lo, hi, rate_tables)
    base_sides, base_totals = side_sums(base_moments, slab_power)
    tables = (decay, green, mark, rows_table(block * rows_run, rows_run), qx_inverse)
    base_rows = solve(
        place, base_f, base_sides, base_totals, wraps, tables, base_a, rows_run, period, 1
    )
    if rows_run != rows_out:
        base_rows = lax.dynamic_slice_in_dim(
            base_rows, mine * rows_out - block * rows_run, rows_out, 2
        )

    part = gram(cells)
    devices = slabs * vectors
    if devices <= 64:
        parts = lax.all_to_all(
            jnp.broadcast_to(part[None], (devices,) + part.shape),
            ("vec", "gz"),
            split_axis=0,
            concat_axis=0,
            tiled=True,
        )
    else:
        parts = lax.psum(part, ("vec", "gz"))[None]
    ortho_cells, growth = ortho(parts, cells, 3.0 * nz * ny * nx)
    returned = lax.all_to_all(ortho_cells, "vec", split_axis=0, concat_axis=0, tiled=True)
    return (base_rows, returned.reshape(tangents.shape), growth[:vectors, 0])


def solution(mesh):
    in_specs = (P(None, "gz", None, None), P("vec", None, "gz", None, None), P())
    out_specs = (P(None, "gz", "vec", None), P("vec", None, "gz", None, None), P())
    return jax.shard_map(
        per_device, mesh=mesh, in_specs=in_specs, out_specs=out_specs, check_vma=False
    )
```

```python
import functools
import math

import jax
import jax.numpy as jnp
import ml_dtypes
import numpy as np
from jax import lax
from jax.experimental import pallas as pl
from jax.experimental.pallas import tpu as pltpu
from jax.sharding import PartitionSpec as P

time_step = 0.005
viscosity = 0.01
forcing_amplitude = 4.0

TILE = 64
SWEEP = 32
LEAST = 16
PAD = 8
MIB = 1024 * 1024


def spacing_of(nx):
    return 2.0 * math.pi / nx


def real_basis(length):
    cells = np.arange(length)
    columns = [np.full(length, 1.0 / np.sqrt(length)), (-1.0) ** cells / np.sqrt(length)]
    waves = [0, length // 2]
    for wave in range(1, length // 2):
        angle = 2.0 * np.pi * ((cells * wave) % length) / length
        columns += [np.sqrt(2.0 / length) * np.cos(angle), np.sqrt(2.0 / length) * np.sin(angle)]
        waves += [wave, wave]
    sines = np.sin(2.0 * np.pi * np.array(waves) / length) ** 2
    sines[:2] = 0.0
    return np.stack(columns, axis=1), sines


def halves(matrix):
    high = matrix.astype(np.float32).astype(ml_dtypes.bfloat16)
    low = (matrix - high.astype(np.float64)).astype(np.float32).astype(ml_dtypes.bfloat16)
    return high, low


def right_table(matrix):
    high, low = halves(matrix)
    return np.concatenate(
        [np.concatenate([high, low], axis=1), np.concatenate([high, low], axis=1)], axis=0
    )


def left_table(matrix):
    high, low = halves(matrix)
    return np.concatenate(
        [np.concatenate([high, high], axis=1), np.concatenate([low, low], axis=1)], axis=0
    )


def column_tables(sines_y, sines_x):
    four = 4.0 * (sines_y[:, None] + sines_x[None, :])
    resting = four == 0.0
    decay = 1.0 / (1.0 + four / 2.0 + np.sqrt(four + four * four / 4.0))
    return decay, resting


def split_cat(data, axis):
    high = data.astype(jnp.bfloat16)
    low = (data - high.astype(jnp.float32)).astype(jnp.bfloat16)
    return jnp.concatenate([high, low], axis=axis)


def right_product(data, table):
    out = jnp.dot(split_cat(data, 1), table, preferred_element_type=jnp.float32)
    width = out.shape[1] // 2
    return out[:, :width] + out[:, width:]


def left_product(table, data):
    out = jnp.dot(table, split_cat(data, 0), preferred_element_type=jnp.float32)
    height = out.shape[0] // 2
    return out[:height] + out[height:]


def power_of(base, exponent):
    out = None
    while exponent > 0:
        if exponent % 2 == 1:
            out = base if out is None else out * base
        base = base * base
        exponent //= 2
    return out


def wrap_rows(ref, index, ny):
    ref[index + (pl.ds(0, PAD),)] = ref[index + (pl.ds(ny, PAD),)]
    ref[index + (pl.ds(ny + PAD, PAD),)] = ref[index + (pl.ds(PAD, PAD),)]


def halo_pairs(source, fields, near, far, inner, sems, side):
    out = []
    for i, (_, ref) in enumerate(fields):
        out += [
            pltpu.make_async_copy(
                source.at[pl.ds(3 * i, 3)], ref.at[:, near, inner], sems.at[side, 2 * i]
            ),
            pltpu.make_async_copy(source.at[6 + i], ref.at[2, far, inner], sems.at[side, 2 * i + 1]),
        ]
    return out


def rate_tile(us, vs, layer, y0, comps):
    nx = vs.shape[3]
    space = spacing_of(nx)
    adv_scale = -time_step / (2.0 * space)
    lap_scale = viscosity * time_step / (space * space)
    rows = pl.ds(PAD + y0, TILE)
    flow = [vs[c, layer, rows] for c in range(3)]
    drift = flow if us is None else [us[c, layer, rows] for c in range(3)]
    out = []

    def neighbours(ref, c, centre):
        return (
            pltpu.roll(centre, nx - 1, 1),
            pltpu.roll(centre, 1, 1),
            ref[c, layer, pl.ds(PAD + y0 + 1, TILE)],
            ref[c, layer, pl.ds(PAD + y0 - 1, TILE)],
            ref[c, layer + 1, rows],
            ref[c, layer - 1, rows],
        )

    for c in comps:
        xp, xm, yp, ym, zp, zm = neighbours(vs if us is None else us, c, drift[c])
        adv = flow[0] * (xp - xm) + flow[1] * (yp - ym) + flow[2] * (zp - zm)
        lap = ((xp + xm) + (yp + ym)) + ((zp + zm) - 6.0 * drift[c])
        if us is not None:
            xp, xm, yp, ym, zp, zm = neighbours(vs, c, flow[c])
            adv = adv + (drift[0] * (xp - xm) + drift[1] * (yp - ym) + drift[2] * (zp - zm))
        out.append(adv_scale * adv + lap_scale * lap)
    return drift, out


def z_rate(fns, layer, slot):
    us, vs, rz = fns[:3]
    for y0 in range(0, rz.shape[1], TILE):
        _, (rate,) = rate_tile(us, vs, layer, y0, (2,))
        rz[slot, pl.ds(y0, TILE)] = rate


def layer_rates(fns, layer, i, shift):
    us, vs, rz, ry, dv, a_out = fns
    ny, nx = rz.shape[1:]
    for y0 in range(0, ny, TILE):
        rows = pl.ds(y0, TILE)
        drift, (rate_x, rate_y) = rate_tile(us, vs, layer, y0, (0, 1))
        if shift is not None:
            rate_x = rate_x + shift
        a_out[0, i, rows] = drift[0] + rate_x
        a_out[1, i, rows] = drift[1] + rate_y
        a_out[2, i, rows] = drift[2] + rz[1, rows]
        dv[i, rows] = pltpu.roll(rate_x, nx - 1, 1) - pltpu.roll(rate_x, 1, 1)
        ry[pl.ds(PAD + y0, TILE)] = rate_y
    z_rate(fns, layer + 1, 2)
    wrap_rows(ry, (), ny)
    for y0 in range(0, ny, TILE):
        rows = pl.ds(y0, TILE)
        along_y = ry[pl.ds(PAD + y0 + 1, TILE)] - ry[pl.ds(PAD + y0 - 1, TILE)]
        middle, upper = rz[1, rows], rz[2, rows]
        along_z = upper - rz[0, rows]
        dv[i, rows] = dv[i, rows] + (along_y + along_z)
        rz[0, rows] = middle
        rz[1, rows] = upper


def transform(dv, f_out, basis, chunk):
    ny, nx = dv.shape[1:]
    qx, qy = basis.at[pl.ds(0, 2 * nx)], basis.at[pl.ds(2 * nx, 2 * ny)]
    waves = right_product(dv[...].reshape(chunk * ny, nx), qx[...]).reshape(chunk, ny, nx)
    waves = left_product(qy[...], jnp.concatenate([waves[i] for i in range(chunk)], axis=1))
    for i in range(chunk):
        f_out[i] = waves[:, i * nx : (i + 1) * nx]


def rate_kernel(tangent, halos, chunk, layers, *refs):
    if tangent:
        (place, u_hbm, v_hbm), refs = refs[:3], refs[3:]
    else:
        (place, profile, v_hbm), refs = refs[:3], refs[3:]
    if halos:
        (lo_hbm, hi_hbm), refs = refs[:2], refs[2:]
    (decay, basis, a_out, f_out, m_out), refs = refs[:5], refs[5:]
    if tangent:
        us, refs = refs[0], refs[1:]
    (vs, rz, ry, dv, pw, sems, halo_sems) = refs
    if not tangent:
        us = vs
    step = pl.program_id(0)
    steps = layers // chunk
    ny = f_out.shape[1]
    fields = [(v_hbm, vs)]
    if tangent:
        fields.append((u_hbm, us))
    inner = pl.ds(PAD, ny)

    def chunk_copies(k):
        return [
            pltpu.make_async_copy(
                source.at[:, pl.ds(k * chunk, chunk)],
                target.at[:, pl.ds(k * chunk + 2, chunk), inner],
                sems.at[k, i],
            )
            for i, (source, target) in enumerate(fields)
        ]

    def halo_copies(side):
        source = (lo_hbm, hi_hbm)[side]
        near, far = ((1, 0), (layers + 2, layers + 3))[side]
        return halo_pairs(source, fields, near, far, inner, halo_sems, side)

    def wait_chunk(k):
        for copy in chunk_copies(k):
            copy.wait()

        def body(i, carry):
            for _, ref in fields:
                for c in range(3):
                    wrap_rows(ref, (c, k * chunk + 2 + i), ny)
            return carry

        lax.fori_loop(0, chunk, body, 0)

    def wait_halo(side):
        for copy in halo_copies(side):
            copy.wait()
        near, far = ((1, 0), (layers + 2, layers + 3))[side]
        for _, ref in fields:
            for c in range(3):
                wrap_rows(ref, (c, near), ny)
            wrap_rows(ref, (2, far), ny)

    fns = (us if tangent else None, vs, rz, ry, dv, a_out)

    @pl.when(step == 0)
    def _():
        if halos:
            for copy in halo_copies(0):
                copy.start()
        for k in range(steps):
            for copy in chunk_copies(k):
                copy.start()
        if halos:
            for copy in halo_copies(1):
                copy.start()
            wait_halo(0)
        wait_chunk(0)
        if halos:
            if steps == 1:
                wait_halo(1)
            z_rate(fns, 1, 0)
            z_rate(fns, 2, 1)
        m_out[...] = jnp.zeros(m_out.shape, jnp.float32)
        start = (place[0] * (layers // 2)).astype(jnp.float32)
        pw[...] = jnp.where(decay[...] >= 1.0, start, 1.0)

    @pl.when(step + 1 < steps)
    def _():
        wait_chunk(step + 1)

    if halos and steps > 1:

        @pl.when(step + 1 == steps)
        def _():
            wait_halo(1)

    for i in range(chunk):
        shift = None if tangent else profile[step * chunk + i]
        layer_rates(fns, step * chunk + i + 2, i, shift)
    transform(dv, f_out, basis, chunk)

    def moments(first, last):
        for y0 in range(0, ny, TILE):
            rows = pl.ds(y0, TILE)
            rate = decay[rows]
            marks = jnp.where(rate >= 1.0, 1.0, 0.0)
            power = pw[rows]
            right = [m_out[0, rows], m_out[1, rows]]
            left = [m_out[2, rows], m_out[3, rows]]
            for i in range(chunk):
                parity = i % 2
                if first <= i < last:
                    f = f_out[i, rows]
                    right[parity] = rate * right[parity] + f
                    left[parity] = left[parity] + power * f
                if parity == 1:
                    power = rate * power + marks
            pw[rows] = power
            m_out[0, rows], m_out[1, rows] = right
            m_out[2, rows], m_out[3, rows] = left

    if halos:
        moments(0, chunk)
    else:
        @pl.when(step == 0)
        def _():
            moments(2, chunk)

        @pl.when((step > 0) & (step + 1 < steps))
        def _():
            moments(0, chunk)

        @pl.when(step + 1 == steps)
        def _():
            moments(0, chunk - 2)


def edge_kernel(layers, *refs):
    (place, u_hbm, v_hbm, lo_hbm, hi_hbm, a_in, f_in, m_in, decay, basis) = refs[:10]
    (a_out, f_out, m_out, us, vs, rz, ry, dv, sems, halo_sems) = refs[10:]
    step = pl.program_id(0)
    ny = f_out.shape[1]
    fields = [(v_hbm, vs), (u_hbm, us)]
    inner = pl.ds(PAD, ny)

    def copies(side):
        source = (lo_hbm, hi_hbm)[side]
        near, far = ((1, 0), (10, 11))[side]
        first, slot = ((0, 2), (layers - 4, 6))[side]
        return halo_pairs(source, fields, near, far, inner, halo_sems, side) + [
            pltpu.make_async_copy(
                ref.at[:, pl.ds(first, 4)], target.at[:, pl.ds(slot, 4), inner], sems.at[side, i]
            )
            for i, (ref, target) in enumerate(fields)
        ]

    def arrive(side):
        for copy in copies(side):
            copy.wait()
        near, far = ((1, 0), (10, 11))[side]
        for _, ref in fields:
            for layer in range(6 * side, 6 * side + 6):
                for c in range(3):
                    if layer != far or c == 2:
                        wrap_rows(ref, (c, layer), ny)

    @pl.when(step == 0)
    def _():
        for side in range(2):
            for copy in copies(side):
                copy.start()
        arrive(0)

    @pl.when(step == 1)
    def _():
        arrive(1)

    fns = (us, vs, rz, ry, dv, a_out)
    top = step * 6 + 2
    z_rate(fns, top - 1, 0)
    z_rate(fns, top, 1)
    for i in range(2):
        layer_rates(fns, top + i, i, None)
    transform(dv, f_out, basis, 2)
    half = layers // 2
    start = place[0] * half
    last = power_of(decay[...], half - 1)

    @pl.when(step == 0)
    def _():
        weight = jnp.where(decay[...] >= 1.0, start.astype(jnp.float32), 1.0)
        for p in range(2):
            m_out[p] = decay[...] * m_in[p] + last * f_out[p]
            m_out[2 + p] = m_in[2 + p] + weight * f_out[p]

    @pl.when(step == 1)
    def _():
        weight = jnp.where(decay[...] >= 1.0, (start + half - 1).astype(jnp.float32), last)
        for p in range(2):
            m_out[p] = m_out[p] + f_out[p]
            m_out[2 + p] = m_out[2 + p] + weight * f_out[p]


def solve_kernel(chunk, layers, period, rows_out, *refs):
    (place, f_in, sides, totals, wrap_l, wrap_r, decay, basis, a_in) = refs[:9]
    (v_out, qm, hat, phi) = refs[9:]
    step = pl.program_id(0)
    ny, nx = f_in.shape[1], f_in.shape[2]
    tall = rows_out + 2 * PAD
    half = layers // 2
    qx, qy = basis.at[pl.ds(0, 2 * nx)], basis.at[pl.ds(2 * nx, 2 * tall)]

    def sweep(y0):
        rows = pl.ds(y0, SWEEP)
        rate = decay[rows]
        resting = rate >= 1.0
        factor = jnp.where(resting, 0.0, -rate / jnp.where(resting, 1.0, 1.0 - rate * rate))
        left = [sides[p, rows] + wrap_l[rows] * totals[p, rows] for p in range(2)]
        right = [sides[2 + p, rows] + wrap_r[rows] * totals[2 + p, rows] for p in range(2)]
        back = list(right)
        for z in reversed(range(layers)):
            f = f_in[z, rows]
            part = rate * back[z % 2]
            qm[z, rows] = part
            back[z % 2] = part + f
        hat[0, rows] = factor * (left[1] + rate * back[1])
        ahead = list(left)
        for z in range(layers):
            ahead[z % 2] = rate * ahead[z % 2] + f_in[z, rows]
            hat[z + 1, rows] = factor * (ahead[z % 2] + qm[z, rows])
        hat[layers + 1, rows] = factor * (rate * ahead[0] + right[0])

    def resting_columns():
        rows = pl.ds(0, PAD)
        marked = decay[rows] >= 1.0
        start = place[0] * half
        for p in range(2):
            own0 = jnp.zeros((PAD, nx), jnp.float32)
            own1 = jnp.zeros((PAD, nx), jnp.float32)
            for j in range(half):
                f = f_in[2 * j + p, rows]
                own0 = own0 + f
                own1 = own1 + (start + j).astype(jnp.float32) * f
            left0 = sides[p, rows]
            right1 = sides[2 + p, rows]
            all0 = totals[p, rows]
            all1 = totals[2 + p, rows]
            right0 = all0 - own0 - left0
            left1 = all1 - own1 - right1
            prefix = jnp.zeros((PAD, nx), jnp.float32)
            twice = jnp.zeros((PAD, nx), jnp.float32)
            first, last = (0, half + 1) if p == 0 else (-1, half)
            for j in range(first, last):
                t = (start + j).astype(jnp.float32)
                if j > 0:
                    twice = twice + prefix
                if 0 <= j < half:
                    prefix = prefix + f_in[2 * j + p, rows]
                value = 0.5 * (t * (left0 - right0 - own0) + (right1 - left1 + own1)) + twice
                value = value - t * (t * all0 - 2.0 * all1) * (0.5 / period)
                z = 2 * j + p + 1
                hat[z, rows] = jnp.where(marked, value, hat[z, rows])

    def invert(first, count, slot):
        cols = jnp.concatenate([hat[first + i] for i in range(count)], axis=1)
        out = left_product(qy[...], cols)
        out = jnp.concatenate([out[:, i * nx : (i + 1) * nx] for i in range(count)], axis=0)
        out = right_product(out, qx[...])
        for i in range(count):
            phi[slot + i] = out[i * tall : (i + 1) * tall]

    @pl.when(step == 0)
    def _():
        def body(i, carry):
            sweep(pl.multiple_of(i * SWEEP, SWEEP))
            return carry

        lax.fori_loop(0, ny // SWEEP, body, 0)
        resting_columns()
        invert(0, 2, 0)

    invert(step * chunk + 2, chunk, 2)

    for i in range(chunk):
        size = min(TILE, rows_out)
        for y0 in range(0, rows_out, size):
            rows = pl.ds(y0, size)
            layer = i + 1
            here = phi[layer, pl.ds(PAD + y0, size)]
            v_out[0, i, rows] = a_in[0, i, rows] - (
                pltpu.roll(here, nx - 1, 1) - pltpu.roll(here, 1, 1)
            )
            v_out[1, i, rows] = a_in[1, i, rows] - (
                phi[layer, pl.ds(PAD + y0 + 1, size)] - phi[layer, pl.ds(PAD + y0 - 1, size)]
            )
            v_out[2, i, rows] = a_in[2, i, rows] - (
                phi[layer + 1, pl.ds(PAD + y0, size)] - phi[layer - 1, pl.ds(PAD + y0, size)]
            )
    for i in range(2):
        phi[i] = phi[chunk + i]


def pairs_of(count):
    return [(i, j) for i in range(count) for j in range(i + 1)]


def gram_kernel(count, x_ref, out_ref, acc):
    step = pl.program_id(0)
    rows = x_ref.shape[1]

    @pl.when(step == 0)
    def _():
        acc[...] = jnp.zeros(acc.shape, jnp.float32)

    group = 8
    for bi in range(0, count, group):
        for bj in range(0, bi + 1, group):
            pairs = [
                (i, j)
                for i in range(bi, min(bi + group, count))
                for j in range(bj, min(bj + group, count))
                if j <= i
            ]
            slots = [i * (i + 1) // 2 + j for i, j in pairs]

            def body(t, sums):
                part = pl.ds(pl.multiple_of(t * 8, 8), 8)
                needed = sorted({i for i, _ in pairs} | {j for _, j in pairs})
                tile = {i: x_ref[i, part] for i in needed}
                return tuple(s + tile[i] * tile[j] for s, (i, j) in zip(sums, pairs))

            sums = lax.fori_loop(0, rows // 8, body, tuple(acc[s] for s in slots), unroll=4)
            for s, value in zip(slots, sums):
                acc[s] = value

    @pl.when(step == pl.num_programs(0) - 1)
    def _():
        shape = out_ref.shape
        row = lax.broadcasted_iota(jnp.int32, shape, 0)
        lane = lax.broadcasted_iota(jnp.int32, shape, 1)
        out = jnp.zeros(shape, jnp.float32)
        for s, (i, j) in enumerate(pairs_of(count)):
            total = jnp.sum(jnp.sum(acc[s], axis=0, keepdims=True), axis=1, keepdims=True)
            for at in {i * count + j, j * count + i}:
                out = jnp.where((row == at // shape[1]) & (lane == at % shape[1]), total, out)
        out_ref[...] = out


def ortho_kernel(count, cells, parts_ref, x_ref, out_ref, growth_ref, coef):
    step = pl.program_id(0)
    rows = x_ref.shape[1]

    @pl.when(step == 0)
    def _():
        nx = x_ref.shape[2]
        shape = (max(8, count), nx)
        row = lax.broadcasted_iota(jnp.int32, shape, 0)
        lane = lax.broadcasted_iota(jnp.int32, shape, 1)
        flat = jnp.sum(parts_ref[...], axis=0) / cells
        work = jnp.where(lane == row + count, 1.0, 0.0)
        for i in range(count):
            at, shift = i * count // nx, i * count % nx
            line = flat[at : at + 1]
            if shift > 0:
                line = pltpu.roll(line, nx - shift, 1)
            work = jnp.where((row == i) & (lane < count), line, work)
        for k in range(count - 1):
            pivot = work[k : k + 1, k : k + 1]
            scale = jnp.where(row[:, :1] > k, work[:, k : k + 1] / pivot, 0.0)
            work = work - scale * work[k : k + 1, :]
        diagonal = jnp.sum(jnp.where(lane == row, work, 0.0), axis=1, keepdims=True)
        growth_ref[...] = jnp.broadcast_to(0.5 * jnp.log(diagonal), shape)
        work = work / jnp.sqrt(diagonal)
        for s, (i, j) in enumerate(pairs_of(count)):
            coef[s] = jnp.broadcast_to(
                work[i : i + 1, count + j : count + j + 1], coef.shape[1:]
            )

    def body(t, carry):
        part = pl.ds(pl.multiple_of(t * 16, 16), 16)
        tile = [x_ref[i, part] for i in range(count)]
        for i in range(count):
            total = None
            for j in range(i + 1):
                c = coef[i * (i + 1) // 2 + j]
                term = jnp.concatenate([c, c], axis=0) * tile[j]
                total = term if total is None else total + term
            out_ref[i, part] = total
        return carry

    lax.fori_loop(0, rows // 16, body, 0, unroll=2)


def params(limit):
    return pltpu.CompilerParams(vmem_limit_bytes=limit * MIB)


def whole(shape):
    return pl.BlockSpec(shape, lambda *_: (0,) * len(shape))


ANY = pl.BlockSpec(memory_space=pl.ANY)
SMEM = pl.BlockSpec(memory_space=pltpu.SMEM)


def rates(place, extra, velocity, halos, tables):
    _, layers, ny, nx = velocity.shape
    tangent = extra.ndim == 4
    chunk = 4 if layers % 4 == 0 else 2
    field = pltpu.VMEM((3, layers + 4, ny + 2 * PAD, nx), jnp.float32)
    scratch = [field, field] if tangent else [field]
    scratch += [
        pltpu.VMEM((3, ny, nx), jnp.float32),
        pltpu.VMEM((ny + 2 * PAD, nx), jnp.float32),
        pltpu.VMEM((chunk, ny, nx), jnp.float32),
        pltpu.VMEM((ny, nx), jnp.float32),
        pltpu.SemaphoreType.DMA((layers // chunk, 2)),
        pltpu.SemaphoreType.DMA((2, 4)),
    ]
    size = velocity.size
    return pl.pallas_call(
        functools.partial(rate_kernel, tangent, len(halos) > 0, chunk, layers),
        grid=(layers // chunk,),
        in_specs=[SMEM, ANY if tangent else SMEM, ANY]
        + [ANY for _ in halos]
        + [whole(t.shape) for t in tables],
        out_specs=[
            pl.BlockSpec((3, chunk, ny, nx), lambda g: (0, g, 0, 0)),
            pl.BlockSpec((chunk, ny, nx), lambda g: (g, 0, 0)),
            whole((4, ny, nx)),
        ],
        out_shape=[
            jax.ShapeDtypeStruct(velocity.shape, jnp.float32),
            jax.ShapeDtypeStruct((layers, ny, nx), jnp.float32),
            jax.ShapeDtypeStruct((4, ny, nx), jnp.float32),
        ],
        scratch_shapes=scratch,
        compiler_params=params(52),
        cost_estimate=pl.CostEstimate(
            flops=60 * size, bytes_accessed=16 * size, transcendentals=0
        ),
        name="tangent_rates" if tangent else "base_rates",
    )(place, extra, velocity, *halos, *tables)


def edge_rates(place, tangent, velocity, halos, a, f, moments, tables):
    _, layers, ny, nx = velocity.shape
    field = pltpu.VMEM((3, 12, ny + 2 * PAD, nx), jnp.float32)
    ends = layers // 2 - 1
    return pl.pallas_call(
        functools.partial(edge_kernel, layers),
        grid=(2,),
        in_specs=[SMEM] + [ANY] * 6 + [whole(t.shape) for t in (moments, *tables)],
        out_specs=[
            pl.BlockSpec((3, 2, ny, nx), lambda g: (0, g * ends, 0, 0)),
            pl.BlockSpec((2, ny, nx), lambda g: (g * ends, 0, 0)),
            whole((4, ny, nx)),
        ],
        out_shape=[
            jax.ShapeDtypeStruct(a.shape, jnp.float32),
            jax.ShapeDtypeStruct(f.shape, jnp.float32),
            jax.ShapeDtypeStruct(moments.shape, jnp.float32),
        ],
        scratch_shapes=[
            field,
            field,
            pltpu.VMEM((3, ny, nx), jnp.float32),
            pltpu.VMEM((ny + 2 * PAD, nx), jnp.float32),
            pltpu.VMEM((2, ny, nx), jnp.float32),
            pltpu.SemaphoreType.DMA((2, 2)),
            pltpu.SemaphoreType.DMA((2, 4)),
        ],
        input_output_aliases={5: 0, 6: 1},
        compiler_params=params(52),
        cost_estimate=pl.CostEstimate(
            flops=60 * 12 * ny * nx, bytes_accessed=160 * ny * nx, transcendentals=0
        ),
        name="tangent_edges",
    )(place, tangent, velocity, *halos, a, f, moments, *tables)


def solve(place, f, sides, totals, wraps, tables, a, rows_out, period, block):
    layers, ny, nx = f.shape
    chunk = 4 if layers % 4 == 0 else 2
    tall = rows_out + 2 * PAD
    moments = whole((4, ny, nx))
    return pl.pallas_call(
        functools.partial(solve_kernel, chunk, layers, period, rows_out),
        grid_spec=pltpu.PrefetchScalarGridSpec(
            num_scalar_prefetch=1,
            grid=(layers // chunk,),
            in_specs=[whole(f.shape), moments, moments, whole((ny, nx)), whole((ny, nx))]
            + [whole(t.shape) for t in tables]
            + [pl.BlockSpec((3, chunk, rows_out, nx), lambda g, p: (0, g, p[1] * block, 0))],
            out_specs=pl.BlockSpec((3, chunk, rows_out, nx), lambda g, p: (0, g, 0, 0)),
            scratch_shapes=[
                pltpu.VMEM((layers, ny, nx), jnp.float32),
                pltpu.VMEM((layers + 2, ny, nx), jnp.float32),
                pltpu.VMEM((chunk + 2, tall, nx), jnp.float32),
            ],
        ),
        out_shape=jax.ShapeDtypeStruct((3, layers, rows_out, nx), jnp.float32),
        compiler_params=params(52),
        cost_estimate=pl.CostEstimate(
            flops=40 * a.size, bytes_accessed=12 * a.size, transcendentals=0
        ),
        name="tangent_solve" if rows_out == ny else "base_solve",
    )(place, f, sides, totals, *wraps, *tables, a)


def row_chunk(rows):
    best = 16
    for size in range(16, 800, 16):
        if rows % size == 0:
            best = size
    return best


def gram(cells):
    count, rows, nx = cells.shape
    size = row_chunk(rows)
    tall = -(-count * count // nx)
    return pl.pallas_call(
        functools.partial(gram_kernel, count),
        grid=(rows // size,),
        in_specs=[pl.BlockSpec((count, size, nx), lambda g: (0, g, 0))],
        out_specs=whole((tall, nx)),
        out_shape=jax.ShapeDtypeStruct((tall, nx), jnp.float32),
        scratch_shapes=[pltpu.VMEM((count * (count + 1) // 2, 8, nx), jnp.float32)],
        compiler_params=params(12),
        cost_estimate=pl.CostEstimate(
            flops=count * cells.size, bytes_accessed=4 * cells.size, transcendentals=0
        ),
        name="gram_parts",
    )(cells)


def ortho(parts, cells, total_cells):
    count, rows, nx = cells.shape
    size = row_chunk(rows)
    return pl.pallas_call(
        functools.partial(ortho_kernel, count, total_cells),
        grid=(rows // size,),
        in_specs=[whole(parts.shape), pl.BlockSpec((count, size, nx), lambda g: (0, g, 0))],
        out_specs=[
            pl.BlockSpec((count, size, nx), lambda g: (0, g, 0)),
            whole((max(8, count), nx)),
        ],
        out_shape=[
            jax.ShapeDtypeStruct(cells.shape, jnp.float32),
            jax.ShapeDtypeStruct((max(8, count), nx), jnp.float32),
        ],
        scratch_shapes=[pltpu.VMEM((count * (count + 1) // 2, 8, nx), jnp.float32)],
        compiler_params=params(20),
        cost_estimate=pl.CostEstimate(
            flops=count * cells.size, bytes_accessed=8 * cells.size, transcendentals=0
        ),
        name="ortho_rows",
    )(parts, cells)


def ring_shift(block, shift):
    count = lax.axis_size("gz")
    return lax.ppermute(block, "gz", [(i, (i + shift) % count) for i in range(count)])


def side_sums(moments, slab_power):
    count = lax.axis_size("gz")
    here = lax.axis_index("gz")
    right, left = moments[:2], moments[2:]
    from_left = jnp.zeros_like(right)
    from_right = jnp.zeros_like(left)
    span = 1
    while span < count:
        swapped = lax.ppermute(
            jnp.concatenate([right, left], axis=0), "gz", [(i, i ^ span) for i in range(count)]
        )
        other_right, other_left = swapped[:2], swapped[2:]
        inside = here % span
        upper = (here // span) % 2 == 1
        to_left = slab_power(inside)
        to_right = slab_power(span - 1 - inside)
        from_left = jnp.where(upper, from_left + to_left * other_right, from_left)
        from_right = jnp.where(upper, from_right, from_right + to_right * other_left)
        across = slab_power(span)
        right = jnp.where(upper, right + across * other_right, other_right + across * right)
        left = jnp.where(upper, other_left + across * left, left + across * other_left)
        span *= 2
    return jnp.concatenate([from_left, from_right], axis=0), jnp.concatenate([right, left], axis=0)


def per_device(base_flow, tangents, shells):
    _, layers, ny, nx = base_flow.shape
    slabs = lax.axis_size("gz")
    vectors = lax.axis_size("vec")
    here = lax.axis_index("gz")
    mine = lax.axis_index("vec")
    nz = slabs * layers
    period = nz // 2
    tangent = tangents[0]

    basis_x, sines_x = real_basis(nx)
    basis_y, sines_y = real_basis(ny)
    decay64, resting = column_tables(sines_y, sines_x)
    decay = jnp.asarray(decay64, jnp.float32)
    slab_log = jnp.asarray((layers // 2) * np.log(decay64), jnp.float32)
    closing = jnp.asarray(
        np.where(resting, 0.0, 1.0 / np.where(resting, 1.0, 1.0 - decay64**period)), jnp.float32
    )

    def slab_power(exponent):
        return jnp.exp(jnp.asarray(exponent).astype(jnp.float32) * slab_log)

    wraps = (closing * slab_power(here), closing * slab_power(slabs - 1 - here))
    forward = jnp.asarray(np.concatenate([right_table(basis_x), left_table(basis_y.T)], axis=0))
    qx_inverse = jnp.asarray(right_table(basis_x.T))
    rows_out = ny // vectors

    def inverse_tables(first, count):
        high, low = halves(np.concatenate([basis_y, basis_y, basis_y], axis=0))
        both = [qx_inverse]
        for part in (high, low):
            part = lax.dynamic_slice_in_dim(jnp.asarray(part), ny + first - PAD, count + 2 * PAD, 0)
            both.append(jnp.concatenate([part, part], axis=1))
        return (decay, jnp.concatenate(both, axis=0))

    def edge(near, far):
        return jnp.concatenate(
            [base_flow[:, near], tangent[:, near], base_flow[2:, far], tangent[2:, far]], axis=0
        )

    lo = ring_shift(edge(layers - 1, layers - 2), 1)
    hi = ring_shift(edge(0, 1), -1)

    rows_run = max(rows_out, LEAST)
    block = mine * rows_out // rows_run
    place = jnp.stack([here, block]).astype(jnp.int32)
    rate_tables = (decay, forward)
    a, f, moments = rates(place, tangent, base_flow, (), rate_tables)
    a, f, moments = edge_rates(place, tangent, base_flow, (lo, hi), a, f, moments, rate_tables)
    sides, totals = side_sums(moments, slab_power)
    tables = inverse_tables(0, ny)
    advanced = solve(place, f, sides, totals, wraps, tables, a, ny, period, 0)
    advanced, base_lo, base_hi = lax.optimization_barrier((advanced, lo, hi))

    piece_rows = 3 * layers * ny // vectors
    cells = lax.all_to_all(
        advanced.reshape(vectors, piece_rows, nx), "vec", split_axis=0, concat_axis=0, tiled=True
    )

    positions = (here * layers + jnp.arange(layers, dtype=jnp.int32)) % nz
    angles = 2.0 * math.pi / nz * (shells[:, None] * positions[None, :] % nz).astype(jnp.float32)
    profile = time_step * forcing_amplitude * jnp.sum(jnp.sin(angles), axis=0)
    base_a, base_f, base_moments = rates(place, profile, base_flow, (base_lo, base_hi), rate_tables)
    base_sides, base_totals = side_sums(base_moments, slab_power)
    tables = inverse_tables(block * rows_run, rows_run)
    base_rows = solve(
        place, base_f, base_sides, base_totals, wraps, tables, base_a, rows_run, period, 1
    )
    if rows_run != rows_out:
        base_rows = lax.dynamic_slice_in_dim(
            base_rows, mine * rows_out - block * rows_run, rows_out, 2
        )

    cells, base_rows = lax.optimization_barrier((cells, base_rows))
    part = gram(cells)
    devices = slabs * vectors
    if devices <= 64:
        parts = lax.all_to_all(
            jnp.broadcast_to(part[None], (devices,) + part.shape),
            ("vec", "gz"),
            split_axis=0,
            concat_axis=0,
            tiled=True,
        )
    else:
        parts = lax.psum(part, ("vec", "gz"))[None]
    ortho_cells, growth = ortho(parts, cells, 3.0 * nz * ny * nx)
    ortho_cells, growth = lax.optimization_barrier((ortho_cells, growth[:vectors, 0]))
    returned = lax.all_to_all(ortho_cells, "vec", split_axis=0, concat_axis=0, tiled=True)
    return (base_rows, returned.reshape(tangents.shape), growth)


def solution(mesh):
    in_specs = (P(None, "gz", None, None), P("vec", None, "gz", None, None), P())
    out_specs = (P(None, "gz", "vec", None), P("vec", None, "gz", None, None), P())
    return jax.shard_map(
        per_device, mesh=mesh, in_specs=in_specs, out_specs=out_specs, check_vma=False
    )
```

```python
import functools
import math

import jax
import jax.numpy as jnp
import ml_dtypes
import numpy as np
from jax import lax
from jax.experimental import pallas as pl
from jax.experimental.pallas import tpu as pltpu
from jax.sharding import PartitionSpec as P

time_step = 0.005
viscosity = 0.01
forcing_amplitude = 4.0

TILE = 128
SWEEP = 32
LEAST = 16
PAD = 8
MIB = 1024 * 1024


def spacing_of(nx):
    return 2.0 * math.pi / nx


def real_basis(length):
    cells = np.arange(length)
    columns = [np.full(length, 1.0 / np.sqrt(length)), (-1.0) ** cells / np.sqrt(length)]
    waves = [0, length // 2]
    for wave in range(1, length // 2):
        angle = 2.0 * np.pi * ((cells * wave) % length) / length
        columns += [np.sqrt(2.0 / length) * np.cos(angle), np.sqrt(2.0 / length) * np.sin(angle)]
        waves += [wave, wave]
    sines = np.sin(2.0 * np.pi * np.array(waves) / length) ** 2
    sines[:2] = 0.0
    return np.stack(columns, axis=1), sines


def halves(matrix):
    high = matrix.astype(np.float32).astype(ml_dtypes.bfloat16)
    low = (matrix - high.astype(np.float64)).astype(np.float32).astype(ml_dtypes.bfloat16)
    return high, low


def right_table(matrix):
    high, low = halves(matrix)
    return np.concatenate(
        [np.concatenate([high, low], axis=1), np.concatenate([high, low], axis=1)], axis=0
    )


def left_table(matrix):
    high, low = halves(matrix)
    return np.concatenate(
        [np.concatenate([high, high], axis=1), np.concatenate([low, low], axis=1)], axis=0
    )


def column_tables(sines_y, sines_x):
    four = 4.0 * (sines_y[:, None] + sines_x[None, :])
    resting = four == 0.0
    decay = 1.0 / (1.0 + four / 2.0 + np.sqrt(four + four * four / 4.0))
    return decay, resting


def split_cat(data, axis):
    high = data.astype(jnp.bfloat16)
    low = (data - high.astype(jnp.float32)).astype(jnp.bfloat16)
    return jnp.concatenate([high, low], axis=axis)


def right_product(data, table):
    out = jnp.dot(split_cat(data, 1), table, preferred_element_type=jnp.float32)
    width = out.shape[1] // 2
    return out[:, :width] + out[:, width:]


def left_product(table, data):
    out = jnp.dot(table, split_cat(data, 0), preferred_element_type=jnp.float32)
    height = out.shape[0] // 2
    return out[:height] + out[height:]


def power_of(base, exponent):
    out = None
    while exponent > 0:
        if exponent % 2 == 1:
            out = base if out is None else out * base
        base = base * base
        exponent //= 2
    return out


def wrap_rows(ref, index, ny):
    ref[index + (pl.ds(0, PAD),)] = ref[index + (pl.ds(ny, PAD),)]
    ref[index + (pl.ds(ny + PAD, PAD),)] = ref[index + (pl.ds(PAD, PAD),)]


def halo_pairs(source, fields, near, far, inner, sems, side):
    out = []
    for i, (_, ref) in enumerate(fields):
        out += [
            pltpu.make_async_copy(
                source.at[pl.ds(3 * i, 3)], ref.at[:, near, inner], sems.at[side, 2 * i]
            ),
            pltpu.make_async_copy(source.at[6 + i], ref.at[2, far, inner], sems.at[side, 2 * i + 1]),
        ]
    return out


def rate_tile(us, vs, layer, y0, comps):
    nx = vs.shape[3]
    space = spacing_of(nx)
    adv_scale = -time_step / (2.0 * space)
    lap_scale = viscosity * time_step / (space * space)
    rows = pl.ds(PAD + y0, TILE)
    flow = [vs[c, layer, rows] for c in range(3)]
    drift = flow if us is None else [us[c, layer, rows] for c in range(3)]
    out = []

    def neighbours(ref, c, centre):
        return (
            pltpu.roll(centre, nx - 1, 1),
            pltpu.roll(centre, 1, 1),
            ref[c, layer, pl.ds(PAD + y0 + 1, TILE)],
            ref[c, layer, pl.ds(PAD + y0 - 1, TILE)],
            ref[c, layer + 1, rows],
            ref[c, layer - 1, rows],
        )

    for c in comps:
        xp, xm, yp, ym, zp, zm = neighbours(vs if us is None else us, c, drift[c])
        adv = flow[0] * (xp - xm) + flow[1] * (yp - ym) + flow[2] * (zp - zm)
        lap = ((xp + xm) + (yp + ym)) + ((zp + zm) - 6.0 * drift[c])
        if us is not None:
            xp, xm, yp, ym, zp, zm = neighbours(vs, c, flow[c])
            adv = adv + (drift[0] * (xp - xm) + drift[1] * (yp - ym) + drift[2] * (zp - zm))
        out.append(adv_scale * adv + lap_scale * lap)
    return drift, out


def z_rate(fns, layer, slot):
    us, vs, rz = fns[:3]
    for y0 in range(0, rz.shape[1], TILE):
        _, (rate,) = rate_tile(us, vs, layer, y0, (2,))
        rz[slot, pl.ds(y0, TILE)] = rate


def layer_rates(fns, layer, i, slot, shift):
    us, vs, rz, ry, dv, a_out = fns
    ny, nx = rz.shape[1:]
    for y0 in range(0, ny, TILE):
        rows = pl.ds(y0, TILE)
        drift, (rate_x, rate_y) = rate_tile(us, vs, layer, y0, (0, 1))
        if shift is not None:
            rate_x = rate_x + shift
        a_out[0, slot, rows] = drift[0] + rate_x
        a_out[1, slot, rows] = drift[1] + rate_y
        a_out[2, slot, rows] = drift[2] + rz[1, rows]
        dv[i, rows] = pltpu.roll(rate_x, nx - 1, 1) - pltpu.roll(rate_x, 1, 1)
        ry[pl.ds(PAD + y0, TILE)] = rate_y
    z_rate(fns, layer + 1, 2)
    wrap_rows(ry, (), ny)
    for y0 in range(0, ny, TILE):
        rows = pl.ds(y0, TILE)
        along_y = ry[pl.ds(PAD + y0 + 1, TILE)] - ry[pl.ds(PAD + y0 - 1, TILE)]
        middle, upper = rz[1, rows], rz[2, rows]
        along_z = upper - rz[0, rows]
        dv[i, rows] = dv[i, rows] + (along_y + along_z)
        rz[0, rows] = middle
        rz[1, rows] = upper


def transform(dv, f_out, basis, chunk):
    ny, nx = dv.shape[1:]
    qx, qy = basis.at[pl.ds(0, 2 * nx)], basis.at[pl.ds(2 * nx, 2 * ny)]
    waves = right_product(dv[...].reshape(chunk * ny, nx), qx[...]).reshape(chunk, ny, nx)
    waves = left_product(qy[...], jnp.concatenate([waves[i] for i in range(chunk)], axis=1))
    for i in range(chunk):
        f_out[i] = waves[:, i * nx : (i + 1) * nx]


def rate_kernel(tangent, halos, chunk, layers, *refs):
    if tangent:
        (place, u_hbm, v_hbm), refs = refs[:3], refs[3:]
    else:
        (place, profile, v_hbm), refs = refs[:3], refs[3:]
    if halos:
        (lo_hbm, hi_hbm), refs = refs[:2], refs[2:]
    (decay_hbm, basis_hbm, a_hbm, f_hbm, m_out), refs = refs[:5], refs[5:]
    if tangent:
        us, refs = refs[0], refs[1:]
    (vs, rz, ry, dv, pw, a_out, f_out, f_all, decay, basis) = refs[:10]
    (sems, halo_sems, out_sems, table_sems) = refs[10:]
    if not tangent:
        us = vs
    step = pl.program_id(0)
    steps = layers // chunk
    ny = f_out.shape[1]
    fields = [(v_hbm, vs)]
    if tangent:
        fields.append((u_hbm, us))
    inner = pl.ds(PAD, ny)

    def chunk_copies(k):
        return [
            pltpu.make_async_copy(
                source.at[:, pl.ds(k * chunk, chunk)],
                target.at[:, pl.ds(k * chunk + 2, chunk), inner],
                sems.at[k, i],
            )
            for i, (source, target) in enumerate(fields)
        ]

    def halo_copies(side):
        source = (lo_hbm, hi_hbm)[side]
        near, far = ((1, 0), (layers + 2, layers + 3))[side]
        return halo_pairs(source, fields, near, far, inner, halo_sems, side)

    def table_copies():
        return [
            pltpu.make_async_copy(decay_hbm, decay, table_sems.at[0]),
            pltpu.make_async_copy(basis_hbm, basis, table_sems.at[1]),
        ]

    def out_copies(k):
        part = pl.ds(k * chunk, chunk)
        return [
            pltpu.make_async_copy(a_out.at[:, part], a_hbm.at[:, part], out_sems.at[k, 0]),
            pltpu.make_async_copy(f_all.at[part], f_hbm.at[part], out_sems.at[k, 1]),
        ]

    def wait_chunk(k):
        for copy in chunk_copies(k):
            copy.wait()

        def body(i, carry):
            for _, ref in fields:
                for c in range(3):
                    wrap_rows(ref, (c, k * chunk + 2 + i), ny)
            return carry

        lax.fori_loop(0, chunk, body, 0)

    def wait_halo(side):
        for copy in halo_copies(side):
            copy.wait()
        near, far = ((1, 0), (layers + 2, layers + 3))[side]
        for _, ref in fields:
            for c in range(3):
                wrap_rows(ref, (c, near), ny)
            wrap_rows(ref, (2, far), ny)

    fns = (us if tangent else None, vs, rz, ry, dv, a_out)

    @pl.when(step == 0)
    def _():
        if halos:
            for copy in halo_copies(0):
                copy.start()
        for k in range(steps):
            for copy in chunk_copies(k):
                copy.start()
            if k == 0:
                for copy in table_copies():
                    copy.start()
        if halos:
            for copy in halo_copies(1):
                copy.start()
            wait_halo(0)
        wait_chunk(0)
        if halos:
            if steps == 1:
                wait_halo(1)
            z_rate(fns, 1, 0)
            z_rate(fns, 2, 1)
        for copy in table_copies():
            copy.wait()
        m_out[...] = jnp.zeros(m_out.shape, jnp.float32)
        start = (place[0] * (layers // 2)).astype(jnp.float32)
        pw[...] = jnp.where(decay[...] >= 1.0, start, 1.0)

    @pl.when(step + 1 < steps)
    def _():
        wait_chunk(step + 1)

    if halos and steps > 1:

        @pl.when(step + 1 == steps)
        def _():
            wait_halo(1)

    for i in range(chunk):
        shift = None if tangent else profile[step * chunk + i]
        layer_rates(fns, step * chunk + i + 2, i, step * chunk + i, shift)
    transform(dv, f_out, basis, chunk)
    for i in range(chunk):
        f_all[step * chunk + i] = f_out[i]
    for copy in out_copies(step):
        copy.start()

    def moments(first, last):
        for y0 in range(0, ny, TILE):
            rows = pl.ds(y0, TILE)
            rate = decay[rows]
            marks = jnp.where(rate >= 1.0, 1.0, 0.0)
            power = pw[rows]
            right = [m_out[0, rows], m_out[1, rows]]
            left = [m_out[2, rows], m_out[3, rows]]
            for i in range(chunk):
                parity = i % 2
                if first <= i < last:
                    f = f_out[i, rows]
                    right[parity] = rate * right[parity] + f
                    left[parity] = left[parity] + power * f
                if parity == 1:
                    power = rate * power + marks
            pw[rows] = power
            m_out[0, rows], m_out[1, rows] = right
            m_out[2, rows], m_out[3, rows] = left

    if halos:
        moments(0, chunk)
    else:
        @pl.when(step == 0)
        def _():
            moments(2, chunk)

        @pl.when((step > 0) & (step + 1 < steps))
        def _():
            moments(0, chunk)

        @pl.when(step + 1 == steps)
        def _():
            moments(0, chunk - 2)

    @pl.when(step + 1 == steps)
    def _():
        for k in range(steps):
            for copy in out_copies(k):
                copy.wait()


def edge_kernel(layers, *refs):
    (place, u_hbm, v_hbm, lo_hbm, hi_hbm, a_in, f_in, m_in, decay_hbm, basis_hbm) = refs[:10]
    (a_out, f_out, m_out, us, vs, rz, ry, dv, decay, basis) = refs[10:20]
    (sems, halo_sems, table_sems) = refs[20:]
    step = pl.program_id(0)
    ny = f_out.shape[1]
    fields = [(v_hbm, vs), (u_hbm, us)]
    inner = pl.ds(PAD, ny)

    def copies(side):
        source = (lo_hbm, hi_hbm)[side]
        near, far = ((1, 0), (10, 11))[side]
        first, slot = ((0, 2), (layers - 4, 6))[side]
        return halo_pairs(source, fields, near, far, inner, halo_sems, side) + [
            pltpu.make_async_copy(
                ref.at[:, pl.ds(first, 4)], target.at[:, pl.ds(slot, 4), inner], sems.at[side, i]
            )
            for i, (ref, target) in enumerate(fields)
        ]

    def arrive(side):
        for copy in copies(side):
            copy.wait()
        near, far = ((1, 0), (10, 11))[side]
        for _, ref in fields:
            for layer in range(6 * side, 6 * side + 6):
                for c in range(3):
                    if layer != far or c == 2:
                        wrap_rows(ref, (c, layer), ny)

    tables = [
        pltpu.make_async_copy(decay_hbm, decay, table_sems.at[0]),
        pltpu.make_async_copy(basis_hbm, basis, table_sems.at[1]),
    ]

    @pl.when(step == 0)
    def _():
        for copy in copies(0) + tables + copies(1):
            copy.start()
        arrive(0)
        for copy in tables:
            copy.wait()

    @pl.when(step == 1)
    def _():
        arrive(1)

    fns = (us, vs, rz, ry, dv, a_out)
    top = step * 6 + 2
    z_rate(fns, top - 1, 0)
    z_rate(fns, top, 1)
    for i in range(2):
        layer_rates(fns, top + i, i, i, None)
    transform(dv, f_out, basis, 2)
    half = layers // 2
    start = place[0] * half
    last = power_of(decay[...], half - 1)

    @pl.when(step == 0)
    def _():
        weight = jnp.where(decay[...] >= 1.0, start.astype(jnp.float32), 1.0)
        for p in range(2):
            m_out[p] = decay[...] * m_in[p] + last * f_out[p]
            m_out[2 + p] = m_in[2 + p] + weight * f_out[p]

    @pl.when(step == 1)
    def _():
        weight = jnp.where(decay[...] >= 1.0, (start + half - 1).astype(jnp.float32), last)
        for p in range(2):
            m_out[p] = m_out[p] + f_out[p]
            m_out[2 + p] = m_out[2 + p] + weight * f_out[p]


def solve_kernel(chunk, layers, period, rows_out, *refs):
    (place, f_hbm, sides, totals, wrap_l, wrap_r, decay, basis, a_hbm) = refs[:9]
    (v_hbm, f_in, av, qm, hat, phi, f_sem, a_sems, v_sems) = refs[9:]
    step = pl.program_id(0)
    steps = layers // chunk
    ny, nx = f_in.shape[1], f_in.shape[2]
    tall = rows_out + 2 * PAD
    half = layers // 2
    qx, qy = basis.at[pl.ds(0, 2 * nx)], basis.at[pl.ds(2 * nx, 2 * tall)]

    def f_copy():
        return pltpu.make_async_copy(f_hbm, f_in, f_sem)

    def a_copy(k):
        part = pl.ds(k * chunk, chunk)
        rows = pl.ds(0, rows_out)
        if rows_out < ny:
            rows = pl.ds(pl.multiple_of(place[1] * rows_out, rows_out), rows_out)
        return pltpu.make_async_copy(a_hbm.at[:, part, rows], av.at[:, part], a_sems.at[k])

    def v_copy(k):
        part = pl.ds(k * chunk, chunk)
        return pltpu.make_async_copy(av.at[:, part], v_hbm.at[:, part], v_sems.at[k])

    def sweep(y0):
        rows = pl.ds(y0, SWEEP)
        rate = decay[rows]
        resting = rate >= 1.0
        factor = jnp.where(resting, 0.0, -rate / jnp.where(resting, 1.0, 1.0 - rate * rate))
        left = [sides[p, rows] + wrap_l[rows] * totals[p, rows] for p in range(2)]
        right = [sides[2 + p, rows] + wrap_r[rows] * totals[2 + p, rows] for p in range(2)]
        back = list(right)
        for z in reversed(range(layers)):
            f = f_in[z, rows]
            part = rate * back[z % 2]
            qm[z, rows] = part
            back[z % 2] = part + f
        hat[0, rows] = factor * (left[1] + rate * back[1])
        ahead = list(left)
        for z in range(layers):
            ahead[z % 2] = rate * ahead[z % 2] + f_in[z, rows]
            hat[z + 1, rows] = factor * (ahead[z % 2] + qm[z, rows])
        hat[layers + 1, rows] = factor * (rate * ahead[0] + right[0])

    def resting_columns():
        rows = pl.ds(0, PAD)
        marked = decay[rows] >= 1.0
        start = place[0] * half
        for p in range(2):
            own0 = jnp.zeros((PAD, nx), jnp.float32)
            own1 = jnp.zeros((PAD, nx), jnp.float32)
            for j in range(half):
                f = f_in[2 * j + p, rows]
                own0 = own0 + f
                own1 = own1 + (start + j).astype(jnp.float32) * f
            left0 = sides[p, rows]
            right1 = sides[2 + p, rows]
            all0 = totals[p, rows]
            all1 = totals[2 + p, rows]
            right0 = all0 - own0 - left0
            left1 = all1 - own1 - right1
            prefix = jnp.zeros((PAD, nx), jnp.float32)
            twice = jnp.zeros((PAD, nx), jnp.float32)
            first, last = (0, half + 1) if p == 0 else (-1, half)
            for j in range(first, last):
                t = (start + j).astype(jnp.float32)
                if j > 0:
                    twice = twice + prefix
                if 0 <= j < half:
                    prefix = prefix + f_in[2 * j + p, rows]
                value = 0.5 * (t * (left0 - right0 - own0) + (right1 - left1 + own1)) + twice
                value = value - t * (t * all0 - 2.0 * all1) * (0.5 / period)
                z = 2 * j + p + 1
                hat[z, rows] = jnp.where(marked, value, hat[z, rows])

    def invert(first, count, slot):
        cols = jnp.concatenate([hat[first + i] for i in range(count)], axis=1)
        out = left_product(qy[...], cols)
        out = jnp.concatenate([out[:, i * nx : (i + 1) * nx] for i in range(count)], axis=0)
        out = right_product(out, qx[...])
        for i in range(count):
            phi[slot + i] = out[i * tall : (i + 1) * tall]

    @pl.when(step == 0)
    def _():
        f_copy().start()
        for k in range(steps):
            a_copy(k).start()
        f_copy().wait()

        def body(i, carry):
            sweep(pl.multiple_of(i * SWEEP, SWEEP))
            return carry

        lax.fori_loop(0, ny // SWEEP, body, 0)
        resting_columns()
        invert(0, 2, 0)

    invert(step * chunk + 2, chunk, 2)
    a_copy(step).wait()

    for i in range(chunk):
        at = step * chunk + i
        size = min(TILE, rows_out)
        for y0 in range(0, rows_out, size):
            rows = pl.ds(y0, size)
            layer = i + 1
            here = phi[layer, pl.ds(PAD + y0, size)]
            av[0, at, rows] = av[0, at, rows] - (
                pltpu.roll(here, nx - 1, 1) - pltpu.roll(here, 1, 1)
            )
            av[1, at, rows] = av[1, at, rows] - (
                phi[layer, pl.ds(PAD + y0 + 1, size)] - phi[layer, pl.ds(PAD + y0 - 1, size)]
            )
            av[2, at, rows] = av[2, at, rows] - (
                phi[layer + 1, pl.ds(PAD + y0, size)] - phi[layer - 1, pl.ds(PAD + y0, size)]
            )
    for i in range(2):
        phi[i] = phi[chunk + i]
    v_copy(step).start()

    @pl.when(step + 1 == steps)
    def _():
        for k in range(steps):
            v_copy(k).wait()


def pairs_of(count):
    return [(i, j) for i in range(count) for j in range(i + 1)]


def gram_kernel(count, x_ref, out_ref, acc):
    step = pl.program_id(0)
    rows = x_ref.shape[1]

    @pl.when(step == 0)
    def _():
        acc[...] = jnp.zeros(acc.shape, jnp.float32)

    group = 8
    for bi in range(0, count, group):
        for bj in range(0, bi + 1, group):
            pairs = [
                (i, j)
                for i in range(bi, min(bi + group, count))
                for j in range(bj, min(bj + group, count))
                if j <= i
            ]
            slots = [i * (i + 1) // 2 + j for i, j in pairs]

            def body(t, sums):
                part = pl.ds(pl.multiple_of(t * 8, 8), 8)
                needed = sorted({i for i, _ in pairs} | {j for _, j in pairs})
                tile = {i: x_ref[i, part] for i in needed}
                return tuple(s + tile[i] * tile[j] for s, (i, j) in zip(sums, pairs))

            sums = lax.fori_loop(0, rows // 8, body, tuple(acc[s] for s in slots), unroll=4)
            for s, value in zip(slots, sums):
                acc[s] = value

    @pl.when(step == pl.num_programs(0) - 1)
    def _():
        shape = out_ref.shape
        row = lax.broadcasted_iota(jnp.int32, shape, 0)
        lane = lax.broadcasted_iota(jnp.int32, shape, 1)
        out = jnp.zeros(shape, jnp.float32)
        for s, (i, j) in enumerate(pairs_of(count)):
            total = jnp.sum(jnp.sum(acc[s], axis=0, keepdims=True), axis=1, keepdims=True)
            for at in {i * count + j, j * count + i}:
                out = jnp.where((row == at // shape[1]) & (lane == at % shape[1]), total, out)
        out_ref[...] = out


def ortho_kernel(count, cells, parts_ref, x_ref, out_ref, growth_ref, coef):
    step = pl.program_id(0)
    rows = x_ref.shape[1]

    @pl.when(step == 0)
    def _():
        nx = x_ref.shape[2]
        shape = (max(8, count), nx)
        row = lax.broadcasted_iota(jnp.int32, shape, 0)
        lane = lax.broadcasted_iota(jnp.int32, shape, 1)
        flat = jnp.sum(parts_ref[...], axis=0) / cells
        work = jnp.where(lane == row + count, 1.0, 0.0)
        for i in range(count):
            at, shift = i * count // nx, i * count % nx
            line = flat[at : at + 1]
            if shift > 0:
                line = pltpu.roll(line, nx - shift, 1)
            work = jnp.where((row == i) & (lane < count), line, work)
        for k in range(count - 1):
            pivot = work[k : k + 1, k : k + 1]
            scale = jnp.where(row[:, :1] > k, work[:, k : k + 1] / pivot, 0.0)
            work = work - scale * work[k : k + 1, :]
        diagonal = jnp.sum(jnp.where(lane == row, work, 0.0), axis=1, keepdims=True)
        growth_ref[...] = jnp.broadcast_to(0.5 * jnp.log(diagonal), shape)
        work = work / jnp.sqrt(diagonal)
        for s, (i, j) in enumerate(pairs_of(count)):
            coef[s] = jnp.broadcast_to(
                work[i : i + 1, count + j : count + j + 1], coef.shape[1:]
            )

    def body(t, carry):
        part = pl.ds(pl.multiple_of(t * 16, 16), 16)
        tile = [x_ref[i, part] for i in range(count)]
        for i in range(count):
            total = None
            for j in range(i + 1):
                c = coef[i * (i + 1) // 2 + j]
                term = jnp.concatenate([c, c], axis=0) * tile[j]
                total = term if total is None else total + term
            out_ref[i, part] = total
        return carry

    lax.fori_loop(0, rows // 16, body, 0, unroll=2)


def params(limit):
    return pltpu.CompilerParams(vmem_limit_bytes=limit * MIB)


def whole(_):
    return pl.BlockSpec(memory_space=pltpu.VMEM)


ANY = pl.BlockSpec(memory_space=pl.ANY)
HBM = pl.BlockSpec(memory_space=pltpu.HBM)
SMEM = pl.BlockSpec(memory_space=pltpu.SMEM)


def rates(place, extra, velocity, halos, tables):
    _, layers, ny, nx = velocity.shape
    tangent = extra.ndim == 4
    chunk = 4 if layers % 4 == 0 else 2
    field = pltpu.VMEM((3, layers + 4, ny + 2 * PAD, nx), jnp.float32)
    scratch = [field, field] if tangent else [field]
    scratch += [
        pltpu.VMEM((3, ny, nx), jnp.float32),
        pltpu.VMEM((ny + 2 * PAD, nx), jnp.float32),
        pltpu.VMEM((chunk, ny, nx), jnp.float32),
        pltpu.VMEM((ny, nx), jnp.float32),
        pltpu.VMEM(velocity.shape, jnp.float32),
        pltpu.VMEM((chunk, ny, nx), jnp.float32),
        pltpu.VMEM((layers, ny, nx), jnp.float32),
        *[pltpu.VMEM(t.shape, t.dtype) for t in tables],
        pltpu.SemaphoreType.DMA((layers // chunk, 2)),
        pltpu.SemaphoreType.DMA((2, 4)),
        pltpu.SemaphoreType.DMA((layers // chunk, 2)),
        pltpu.SemaphoreType.DMA((2,)),
    ]
    size = velocity.size
    return pl.pallas_call(
        functools.partial(rate_kernel, tangent, len(halos) > 0, chunk, layers),
        grid=(layers // chunk,),
        in_specs=[SMEM, ANY if tangent else SMEM, ANY]
        + [ANY for _ in halos]
        + [HBM for _ in tables],
        out_specs=[ANY, ANY, whole((4, ny, nx))],
        out_shape=[
            jax.ShapeDtypeStruct(velocity.shape, jnp.float32),
            jax.ShapeDtypeStruct((layers, ny, nx), jnp.float32),
            jax.ShapeDtypeStruct((4, ny, nx), jnp.float32),
        ],
        scratch_shapes=scratch,
        compiler_params=params(52 if tangent else 28),
        cost_estimate=pl.CostEstimate(
            flops=60 * size, bytes_accessed=16 * size, transcendentals=0
        ),
        name="tangent_rates" if tangent else "base_rates",
    )(place, extra, velocity, *halos, *tables)


def edge_rates(place, tangent, velocity, halos, a, f, moments, tables):
    _, layers, ny, nx = velocity.shape
    field = pltpu.VMEM((3, 12, ny + 2 * PAD, nx), jnp.float32)
    ends = layers // 2 - 1
    return pl.pallas_call(
        functools.partial(edge_kernel, layers),
        grid=(2,),
        in_specs=[SMEM] + [ANY] * 6 + [whole(moments.shape)] + [HBM for _ in tables],
        out_specs=[
            pl.BlockSpec((3, 2, ny, nx), lambda g: (0, g * ends, 0, 0)),
            pl.BlockSpec((2, ny, nx), lambda g: (g * ends, 0, 0)),
            whole((4, ny, nx)),
        ],
        out_shape=[
            jax.ShapeDtypeStruct(a.shape, jnp.float32),
            jax.ShapeDtypeStruct(f.shape, jnp.float32),
            jax.ShapeDtypeStruct(moments.shape, jnp.float32),
        ],
        scratch_shapes=[
            field,
            field,
            pltpu.VMEM((3, ny, nx), jnp.float32),
            pltpu.VMEM((ny + 2 * PAD, nx), jnp.float32),
            pltpu.VMEM((2, ny, nx), jnp.float32),
            *[pltpu.VMEM(t.shape, t.dtype) for t in tables],
            pltpu.SemaphoreType.DMA((2, 2)),
            pltpu.SemaphoreType.DMA((2, 4)),
            pltpu.SemaphoreType.DMA((2,)),
        ],
        input_output_aliases={5: 0, 6: 1},
        compiler_params=params(52),
        cost_estimate=pl.CostEstimate(
            flops=60 * 12 * ny * nx, bytes_accessed=160 * ny * nx, transcendentals=0
        ),
        name="tangent_edges",
    )(place, tangent, velocity, *halos, a, f, moments, *tables)


def solve(place, f, sides, totals, wraps, tables, a, rows_out, period):
    layers, ny, nx = f.shape
    chunk = 8 if layers % 8 == 0 else 2
    tall = rows_out + 2 * PAD
    moments = whole((4, ny, nx))
    return pl.pallas_call(
        functools.partial(solve_kernel, chunk, layers, period, rows_out),
        grid_spec=pltpu.PrefetchScalarGridSpec(
            num_scalar_prefetch=1,
            grid=(layers // chunk,),
            in_specs=[ANY, moments, moments, whole((ny, nx)), whole((ny, nx))]
            + [whole(t.shape) for t in tables]
            + [ANY],
            out_specs=ANY,
            scratch_shapes=[
                pltpu.VMEM((layers, ny, nx), jnp.float32),
                pltpu.VMEM((3, layers, rows_out, nx), jnp.float32),
                pltpu.VMEM((layers, ny, nx), jnp.float32),
                pltpu.VMEM((layers + 2, ny, nx), jnp.float32),
                pltpu.VMEM((chunk + 2, tall, nx), jnp.float32),
                pltpu.SemaphoreType.DMA,
                pltpu.SemaphoreType.DMA((layers // chunk,)),
                pltpu.SemaphoreType.DMA((layers // chunk,)),
            ],
        ),
        out_shape=jax.ShapeDtypeStruct((3, layers, rows_out, nx), jnp.float32),
        compiler_params=params(52 if rows_out == ny else 16),
        cost_estimate=pl.CostEstimate(
            flops=40 * a.size, bytes_accessed=12 * a.size, transcendentals=0
        ),
        name="tangent_solve" if rows_out == ny else "base_solve",
    )(place, f, sides, totals, *wraps, *tables, a)


def row_chunk(rows):
    best = 16
    for size in range(16, 800, 16):
        if rows % size == 0:
            best = size
    return best


def gram(cells):
    count, rows, nx = cells.shape
    size = row_chunk(rows)
    tall = -(-count * count // nx)
    return pl.pallas_call(
        functools.partial(gram_kernel, count),
        grid=(rows // size,),
        in_specs=[pl.BlockSpec((count, size, nx), lambda g: (0, g, 0))],
        out_specs=whole((tall, nx)),
        out_shape=jax.ShapeDtypeStruct((tall, nx), jnp.float32),
        scratch_shapes=[pltpu.VMEM((count * (count + 1) // 2, 8, nx), jnp.float32)],
        compiler_params=params(12),
        cost_estimate=pl.CostEstimate(
            flops=count * cells.size, bytes_accessed=4 * cells.size, transcendentals=0
        ),
        name="gram_parts",
    )(cells)


def ortho(parts, cells, total_cells):
    count, rows, nx = cells.shape
    size = row_chunk(rows)
    return pl.pallas_call(
        functools.partial(ortho_kernel, count, total_cells),
        grid=(rows // size,),
        in_specs=[whole(parts.shape), pl.BlockSpec((count, size, nx), lambda g: (0, g, 0))],
        out_specs=[
            pl.BlockSpec((count, size, nx), lambda g: (0, g, 0)),
            whole((max(8, count), nx)),
        ],
        out_shape=[
            jax.ShapeDtypeStruct(cells.shape, jnp.float32),
            jax.ShapeDtypeStruct((max(8, count), nx), jnp.float32),
        ],
        scratch_shapes=[pltpu.VMEM((count * (count + 1) // 2, 8, nx), jnp.float32)],
        compiler_params=params(20),
        cost_estimate=pl.CostEstimate(
            flops=count * cells.size, bytes_accessed=8 * cells.size, transcendentals=0
        ),
        name="ortho_rows",
    )(parts, cells)


def ring_shift(block, shift):
    count = lax.axis_size("gz")
    return lax.ppermute(block, "gz", [(i, (i + shift) % count) for i in range(count)])


def side_sums(moments, slab_power):
    count = lax.axis_size("gz")
    here = lax.axis_index("gz")
    right, left = moments[:2], moments[2:]
    from_left = jnp.zeros_like(right)
    from_right = jnp.zeros_like(left)
    span = 1
    while span < count:
        swapped = lax.ppermute(
            jnp.concatenate([right, left], axis=0), "gz", [(i, i ^ span) for i in range(count)]
        )
        other_right, other_left = swapped[:2], swapped[2:]
        inside = here % span
        upper = (here // span) % 2 == 1
        to_left = slab_power(inside)
        to_right = slab_power(span - 1 - inside)
        from_left = jnp.where(upper, from_left + to_left * other_right, from_left)
        from_right = jnp.where(upper, from_right, from_right + to_right * other_left)
        across = slab_power(span)
        right = jnp.where(upper, right + across * other_right, other_right + across * right)
        left = jnp.where(upper, other_left + across * left, left + across * other_left)
        span *= 2
    return jnp.concatenate([from_left, from_right], axis=0), jnp.concatenate([right, left], axis=0)


def per_device(base_flow, tangents, shells):
    _, layers, ny, nx = base_flow.shape
    slabs = lax.axis_size("gz")
    vectors = lax.axis_size("vec")
    here = lax.axis_index("gz")
    mine = lax.axis_index("vec")
    nz = slabs * layers
    period = nz // 2
    tangent = tangents[0]

    basis_x, sines_x = real_basis(nx)
    basis_y, sines_y = real_basis(ny)
    decay64, resting = column_tables(sines_y, sines_x)
    decay = jnp.asarray(decay64, jnp.float32)
    slab_log = jnp.asarray((layers // 2) * np.log(decay64), jnp.float32)
    closing = jnp.asarray(
        np.where(resting, 0.0, 1.0 / np.where(resting, 1.0, 1.0 - decay64**period)), jnp.float32
    )

    def slab_power(exponent):
        return jnp.exp(jnp.asarray(exponent).astype(jnp.float32) * slab_log)

    wraps = (closing * slab_power(here), closing * slab_power(slabs - 1 - here))
    forward = jnp.asarray(np.concatenate([right_table(basis_x), left_table(basis_y.T)], axis=0))
    qx_inverse = jnp.asarray(right_table(basis_x.T))
    rows_out = ny // vectors

    def inverse_tables(first, count):
        high, low = halves(np.concatenate([basis_y, basis_y, basis_y], axis=0))
        both = [qx_inverse]
        for part in (high, low):
            part = lax.dynamic_slice_in_dim(jnp.asarray(part), ny + first - PAD, count + 2 * PAD, 0)
            both.append(jnp.concatenate([part, part], axis=1))
        return (decay, jnp.concatenate(both, axis=0))

    def edge(near, far):
        return jnp.concatenate(
            [base_flow[:, near], tangent[:, near], base_flow[2:, far], tangent[2:, far]], axis=0
        )

    lo = ring_shift(edge(layers - 1, layers - 2), 1)
    hi = ring_shift(edge(0, 1), -1)

    rows_run = max(rows_out, LEAST)
    block = mine * rows_out // rows_run
    place = jnp.stack([here, block]).astype(jnp.int32)
    rate_tables = (decay, forward)
    a, f, moments = rates(place, tangent, base_flow, (), rate_tables)
    a, f, moments = edge_rates(place, tangent, base_flow, (lo, hi), a, f, moments, rate_tables)
    sides, totals = side_sums(moments, slab_power)
    tables = inverse_tables(0, ny)
    advanced = solve(place, f, sides, totals, wraps, tables, a, ny, period)
    advanced, base_lo, base_hi = lax.optimization_barrier((advanced, lo, hi))

    piece_rows = 3 * layers * ny // vectors
    cells = lax.all_to_all(
        advanced.reshape(vectors, piece_rows, nx), "vec", split_axis=0, concat_axis=0, tiled=True
    )

    positions = (here * layers + jnp.arange(layers, dtype=jnp.int32)) % nz
    angles = 2.0 * math.pi / nz * (shells[:, None] * positions[None, :] % nz).astype(jnp.float32)
    profile = time_step * forcing_amplitude * jnp.sum(jnp.sin(angles), axis=0)
    base_a, base_f, base_moments = rates(place, profile, base_flow, (base_lo, base_hi), rate_tables)
    base_sides, base_totals = side_sums(base_moments, slab_power)
    tables = inverse_tables(block * rows_run, rows_run)
    base_rows = solve(
        place, base_f, base_sides, base_totals, wraps, tables, base_a, rows_run, period
    )
    if rows_run != rows_out:
        base_rows = lax.dynamic_slice_in_dim(
            base_rows, mine * rows_out - block * rows_run, rows_out, 2
        )

    cells, base_rows = lax.optimization_barrier((cells, base_rows))
    part = gram(cells)
    devices = slabs * vectors
    if devices <= 64:
        parts = lax.all_to_all(
            jnp.broadcast_to(part[None], (devices,) + part.shape),
            ("vec", "gz"),
            split_axis=0,
            concat_axis=0,
            tiled=True,
        )
    else:
        parts = lax.psum(part, ("vec", "gz"))[None]
    ortho_cells, growth = ortho(parts, cells, 3.0 * nz * ny * nx)
    ortho_cells, growth = lax.optimization_barrier((ortho_cells, growth[:vectors, 0]))
    returned = lax.all_to_all(ortho_cells, "vec", split_axis=0, concat_axis=0, tiled=True)
    return (base_rows, returned.reshape(tangents.shape), growth)


def solution(mesh):
    in_specs = (P(None, "gz", None, None), P("vec", None, "gz", None, None), P())
    out_specs = (P(None, "gz", "vec", None), P("vec", None, "gz", None, None), P())
    return jax.shard_map(
        per_device, mesh=mesh, in_specs=in_specs, out_specs=out_specs, check_vma=False
    )
```

```python
import functools
import math

import jax
import jax.numpy as jnp
import ml_dtypes
import numpy as np
from jax import lax
from jax.experimental import pallas as pl
from jax.experimental.pallas import tpu as pltpu
from jax.sharding import PartitionSpec as P

time_step = 0.005
viscosity = 0.01
forcing_amplitude = 4.0

TILE = 128
SWEEP = 32
LEAST = 16
PAD = 8
MIB = 1024 * 1024


def spacing_of(nx):
    return 2.0 * math.pi / nx


def real_basis(length):
    cells = np.arange(length)
    columns = [np.full(length, 1.0 / np.sqrt(length)), (-1.0) ** cells / np.sqrt(length)]
    waves = [0, length // 2]
    for wave in range(1, length // 2):
        angle = 2.0 * np.pi * ((cells * wave) % length) / length
        columns += [np.sqrt(2.0 / length) * np.cos(angle), np.sqrt(2.0 / length) * np.sin(angle)]
        waves += [wave, wave]
    sines = np.sin(2.0 * np.pi * np.array(waves) / length) ** 2
    sines[:2] = 0.0
    return np.stack(columns, axis=1), sines


def halves(matrix):
    high = matrix.astype(np.float32).astype(ml_dtypes.bfloat16)
    low = (matrix - high.astype(np.float64)).astype(np.float32).astype(ml_dtypes.bfloat16)
    return high, low


def right_table(matrix):
    high, low = halves(matrix)
    return np.concatenate(
        [np.concatenate([high, low], axis=1), np.concatenate([high, low], axis=1)], axis=0
    )


def left_table(matrix):
    high, low = halves(matrix)
    return np.concatenate(
        [np.concatenate([high, high], axis=1), np.concatenate([low, low], axis=1)], axis=0
    )


def column_tables(sines_y, sines_x):
    four = 4.0 * (sines_y[:, None] + sines_x[None, :])
    resting = four == 0.0
    decay = 1.0 / (1.0 + four / 2.0 + np.sqrt(four + four * four / 4.0))
    return decay, resting


def split_cat(data, axis):
    high = data.astype(jnp.bfloat16)
    low = (data - high.astype(jnp.float32)).astype(jnp.bfloat16)
    return jnp.concatenate([high, low], axis=axis)


def right_product(data, table):
    out = jnp.dot(split_cat(data, 1), table, preferred_element_type=jnp.float32)
    width = out.shape[1] // 2
    return out[:, :width] + out[:, width:]


def left_product(table, data):
    out = jnp.dot(table, split_cat(data, 0), preferred_element_type=jnp.float32)
    height = out.shape[0] // 2
    return out[:height] + out[height:]


def power_of(base, exponent):
    out = None
    while exponent > 0:
        if exponent % 2 == 1:
            out = base if out is None else out * base
        base = base * base
        exponent //= 2
    return out


def wrap_rows(ref, index, ny):
    ref[index + (pl.ds(0, PAD),)] = ref[index + (pl.ds(ny, PAD),)]
    ref[index + (pl.ds(ny + PAD, PAD),)] = ref[index + (pl.ds(PAD, PAD),)]


def halo_pairs(source, fields, near, far, inner, sems, side):
    out = []
    for i, (_, ref) in enumerate(fields):
        out += [
            pltpu.make_async_copy(
                source.at[pl.ds(3 * i, 3)], ref.at[:, near, inner], sems.at[side, 2 * i]
            ),
            pltpu.make_async_copy(source.at[6 + i], ref.at[2, far, inner], sems.at[side, 2 * i + 1]),
        ]
    return out


def rate_tile(us, vs, layer, y0, comps):
    nx = vs.shape[3]
    space = spacing_of(nx)
    adv_scale = -time_step / (2.0 * space)
    lap_scale = viscosity * time_step / (space * space)
    rows = pl.ds(PAD + y0, TILE)
    flow = [vs[c, layer, rows] for c in range(3)]
    drift = flow if us is None else [us[c, layer, rows] for c in range(3)]
    out = []

    def neighbours(ref, c, centre):
        return (
            pltpu.roll(centre, nx - 1, 1),
            pltpu.roll(centre, 1, 1),
            ref[c, layer, pl.ds(PAD + y0 + 1, TILE)],
            ref[c, layer, pl.ds(PAD + y0 - 1, TILE)],
            ref[c, layer + 1, rows],
            ref[c, layer - 1, rows],
        )

    for c in comps:
        xp, xm, yp, ym, zp, zm = neighbours(vs if us is None else us, c, drift[c])
        adv = flow[0] * (xp - xm) + flow[1] * (yp - ym) + flow[2] * (zp - zm)
        lap = ((xp + xm) + (yp + ym)) + ((zp + zm) - 6.0 * drift[c])
        if us is not None:
            xp, xm, yp, ym, zp, zm = neighbours(vs, c, flow[c])
            adv = adv + (drift[0] * (xp - xm) + drift[1] * (yp - ym) + drift[2] * (zp - zm))
        out.append(adv_scale * adv + lap_scale * lap)
    return drift, out


def z_rate(fns, layer, slot):
    us, vs, rz = fns[:3]
    for y0 in range(0, rz.shape[1], TILE):
        _, (rate,) = rate_tile(us, vs, layer, y0, (2,))
        rz[slot, pl.ds(y0, TILE)] = rate


def layer_rates(fns, layer, i, slot, shift):
    us, vs, rz, ry, dv, a_out = fns
    ny, nx = rz.shape[1:]
    for y0 in range(0, ny, TILE):
        rows = pl.ds(y0, TILE)
        drift, (rate_x, rate_y) = rate_tile(us, vs, layer, y0, (0, 1))
        if shift is not None:
            rate_x = rate_x + shift
        a_out[0, slot, rows] = drift[0] + rate_x
        a_out[1, slot, rows] = drift[1] + rate_y
        a_out[2, slot, rows] = drift[2] + rz[1, rows]
        dv[i, rows] = pltpu.roll(rate_x, nx - 1, 1) - pltpu.roll(rate_x, 1, 1)
        ry[pl.ds(PAD + y0, TILE)] = rate_y
    z_rate(fns, layer + 1, 2)
    wrap_rows(ry, (), ny)
    for y0 in range(0, ny, TILE):
        rows = pl.ds(y0, TILE)
        along_y = ry[pl.ds(PAD + y0 + 1, TILE)] - ry[pl.ds(PAD + y0 - 1, TILE)]
        middle, upper = rz[1, rows], rz[2, rows]
        along_z = upper - rz[0, rows]
        dv[i, rows] = dv[i, rows] + (along_y + along_z)
        rz[0, rows] = middle
        rz[1, rows] = upper


def transform(dv, f_out, basis, chunk):
    ny, nx = dv.shape[1:]
    qx, qy = basis.at[pl.ds(0, 2 * nx)], basis.at[pl.ds(2 * nx, 2 * ny)]
    waves = right_product(dv[...].reshape(chunk * ny, nx), qx[...]).reshape(chunk, ny, nx)
    waves = left_product(qy[...], jnp.concatenate([waves[i] for i in range(chunk)], axis=1))
    for i in range(chunk):
        f_out[i] = waves[:, i * nx : (i + 1) * nx]


def rate_kernel(tangent, halos, chunk, layers, *refs):
    if tangent:
        (place, u_hbm, v_hbm), refs = refs[:3], refs[3:]
    else:
        (place, profile, v_hbm), refs = refs[:3], refs[3:]
    if halos:
        (lo_hbm, hi_hbm), refs = refs[:2], refs[2:]
    (decay_hbm, basis_hbm, a_hbm, f_hbm, m_out), refs = refs[:5], refs[5:]
    if tangent:
        us, refs = refs[0], refs[1:]
    (vs, rz, ry, dv, pw, a_out, f_out, f_all, decay, basis) = refs[:10]
    (sems, halo_sems, out_sems, table_sems) = refs[10:]
    if not tangent:
        us = vs
    step = pl.program_id(0)
    steps = layers // chunk
    ny = f_out.shape[1]
    fields = [(v_hbm, vs)]
    if tangent:
        fields.append((u_hbm, us))
    inner = pl.ds(PAD, ny)

    def chunk_copies(k):
        return [
            pltpu.make_async_copy(
                source.at[:, pl.ds(k * chunk, chunk)],
                target.at[:, pl.ds(k * chunk + 2, chunk), inner],
                sems.at[k, i],
            )
            for i, (source, target) in enumerate(fields)
        ]

    def halo_copies(side):
        source = (lo_hbm, hi_hbm)[side]
        near, far = ((1, 0), (layers + 2, layers + 3))[side]
        return halo_pairs(source, fields, near, far, inner, halo_sems, side)

    def table_copies():
        return [
            pltpu.make_async_copy(decay_hbm, decay, table_sems.at[0]),
            pltpu.make_async_copy(basis_hbm, basis, table_sems.at[1]),
        ]

    def out_copies(k):
        part = pl.ds(k * chunk, chunk)
        return [
            pltpu.make_async_copy(a_out.at[:, part], a_hbm.at[:, part], out_sems.at[k, 0]),
            pltpu.make_async_copy(f_all.at[part], f_hbm.at[part], out_sems.at[k, 1]),
        ]

    def wait_chunk(k):
        for copy in chunk_copies(k):
            copy.wait()

        def body(i, carry):
            for _, ref in fields:
                for c in range(3):
                    wrap_rows(ref, (c, k * chunk + 2 + i), ny)
            return carry

        lax.fori_loop(0, chunk, body, 0)

    def wait_halo(side):
        for copy in halo_copies(side):
            copy.wait()
        near, far = ((1, 0), (layers + 2, layers + 3))[side]
        for _, ref in fields:
            for c in range(3):
                wrap_rows(ref, (c, near), ny)
            wrap_rows(ref, (2, far), ny)

    fns = (us if tangent else None, vs, rz, ry, dv, a_out)

    @pl.when(step == 0)
    def _():
        if halos:
            for copy in halo_copies(0):
                copy.start()
        for k in range(steps):
            for copy in chunk_copies(k):
                copy.start()
            if k == 0:
                for copy in table_copies():
                    copy.start()
        if halos:
            for copy in halo_copies(1):
                copy.start()
            wait_halo(0)
        wait_chunk(0)
        if halos:
            if steps == 1:
                wait_halo(1)
            z_rate(fns, 1, 0)
            z_rate(fns, 2, 1)
        for copy in table_copies():
            copy.wait()
        m_out[...] = jnp.zeros(m_out.shape, jnp.float32)
        start = (place[0] * (layers // 2)).astype(jnp.float32)
        pw[...] = jnp.where(decay[...] >= 1.0, start, 1.0)

    @pl.when(step + 1 < steps)
    def _():
        wait_chunk(step + 1)

    if halos and steps > 1:

        @pl.when(step + 1 == steps)
        def _():
            wait_halo(1)

    for i in range(chunk):
        shift = None if tangent else profile[step * chunk + i]
        layer_rates(fns, step * chunk + i + 2, i, step * chunk + i, shift)
    transform(dv, f_out, basis, chunk)
    for i in range(chunk):
        f_all[step * chunk + i] = f_out[i]
    for copy in out_copies(step):
        copy.start()

    for y0 in range(0, ny, TILE):
        rows = pl.ds(y0, TILE)
        rate = decay[rows]
        marks = jnp.where(rate >= 1.0, 1.0, 0.0)
        power = pw[rows]
        right = [m_out[0, rows], m_out[1, rows]]
        left = [m_out[2, rows], m_out[3, rows]]
        for i in range(chunk):
            parity = i % 2
            f = f_out[i, rows]
            ahead = rate * right[parity] + f
            if not halos:
                if i < 2:
                    f = jnp.where(step > 0, f, 0.0)
                    ahead = rate * right[parity] + f
                if i >= chunk - 2:
                    f = jnp.where(step + 1 < steps, f, 0.0)
                    ahead = jnp.where(step + 1 < steps, ahead, right[parity])
            right[parity] = ahead
            left[parity] = left[parity] + power * f
            if parity == 1:
                power = rate * power + marks
        pw[rows] = power
        m_out[0, rows], m_out[1, rows] = right
        m_out[2, rows], m_out[3, rows] = left

    @pl.when(step + 1 == steps)
    def _():
        for k in range(steps):
            for copy in out_copies(k):
                copy.wait()


def edge_kernel(layers, *refs):
    (place, u_hbm, v_hbm, lo_hbm, hi_hbm, a_in, f_in, m_in, decay_hbm, basis_hbm) = refs[:10]
    (a_out, f_out, m_out, us, vs, rz, ry, dv, decay, basis) = refs[10:20]
    (sems, halo_sems, table_sems) = refs[20:]
    step = pl.program_id(0)
    ny = f_out.shape[1]
    fields = [(v_hbm, vs), (u_hbm, us)]
    inner = pl.ds(PAD, ny)

    def copies(side):
        source = (lo_hbm, hi_hbm)[side]
        near, far = ((1, 0), (10, 11))[side]
        first, slot = ((0, 2), (layers - 4, 6))[side]
        return halo_pairs(source, fields, near, far, inner, halo_sems, side) + [
            pltpu.make_async_copy(
                ref.at[:, pl.ds(first, 4)], target.at[:, pl.ds(slot, 4), inner], sems.at[side, i]
            )
            for i, (ref, target) in enumerate(fields)
        ]

    def arrive(side):
        for copy in copies(side):
            copy.wait()
        near, far = ((1, 0), (10, 11))[side]
        for _, ref in fields:
            for layer in range(6 * side, 6 * side + 6):
                for c in range(3):
                    if layer != far or c == 2:
                        wrap_rows(ref, (c, layer), ny)

    tables = [
        pltpu.make_async_copy(decay_hbm, decay, table_sems.at[0]),
        pltpu.make_async_copy(basis_hbm, basis, table_sems.at[1]),
    ]

    @pl.when(step == 0)
    def _():
        for copy in copies(0) + tables + copies(1):
            copy.start()
        arrive(0)
        for copy in tables:
            copy.wait()

    @pl.when(step == 1)
    def _():
        arrive(1)

    fns = (us, vs, rz, ry, dv, a_out)
    top = step * 6 + 2
    z_rate(fns, top - 1, 0)
    z_rate(fns, top, 1)
    for i in range(2):
        layer_rates(fns, top + i, i, i, None)
    transform(dv, f_out, basis, 2)
    half = layers // 2
    start = place[0] * half
    last = power_of(decay[...], half - 1)

    @pl.when(step == 0)
    def _():
        weight = jnp.where(decay[...] >= 1.0, start.astype(jnp.float32), 1.0)
        for p in range(2):
            m_out[p] = decay[...] * m_in[p] + last * f_out[p]
            m_out[2 + p] = m_in[2 + p] + weight * f_out[p]

    @pl.when(step == 1)
    def _():
        weight = jnp.where(decay[...] >= 1.0, (start + half - 1).astype(jnp.float32), last)
        for p in range(2):
            m_out[p] = m_out[p] + f_out[p]
            m_out[2 + p] = m_out[2 + p] + weight * f_out[p]


def solve_kernel(chunk, layers, period, rows_out, *refs):
    (place, f_hbm, sides, totals, wrap_l, wrap_r, decay, basis, a_hbm) = refs[:9]
    (v_hbm, f_in, av, qm, hat, phi, f_sem, a_sems, v_sems) = refs[9:]
    step = pl.program_id(0)
    steps = layers // chunk
    ny, nx = f_in.shape[1], f_in.shape[2]
    tall = rows_out + 2 * PAD
    half = layers // 2
    qx, qy = basis.at[pl.ds(0, 2 * nx)], basis.at[pl.ds(2 * nx, 2 * tall)]

    def f_copy():
        return pltpu.make_async_copy(f_hbm, f_in, f_sem)

    def a_copy(k):
        part = pl.ds(k * chunk, chunk)
        rows = pl.ds(0, rows_out)
        if rows_out < ny:
            rows = pl.ds(pl.multiple_of(place[1] * rows_out, rows_out), rows_out)
        return pltpu.make_async_copy(a_hbm.at[:, part, rows], av.at[:, part], a_sems.at[k])

    def v_copy(k):
        part = pl.ds(k * chunk, chunk)
        return pltpu.make_async_copy(av.at[:, part], v_hbm.at[:, part], v_sems.at[k])

    def sweep(y0):
        rows = pl.ds(y0, SWEEP)
        rate = decay[rows]
        resting = rate >= 1.0
        factor = jnp.where(resting, 0.0, -rate / jnp.where(resting, 1.0, 1.0 - rate * rate))
        left = [sides[p, rows] + wrap_l[rows] * totals[p, rows] for p in range(2)]
        right = [sides[2 + p, rows] + wrap_r[rows] * totals[2 + p, rows] for p in range(2)]
        back = list(right)
        for z in reversed(range(layers)):
            f = f_in[z, rows]
            part = rate * back[z % 2]
            qm[z, rows] = part
            back[z % 2] = part + f
        hat[0, rows] = factor * (left[1] + rate * back[1])
        ahead = list(left)
        for z in range(layers):
            ahead[z % 2] = rate * ahead[z % 2] + f_in[z, rows]
            hat[z + 1, rows] = factor * (ahead[z % 2] + qm[z, rows])
        hat[layers + 1, rows] = factor * (rate * ahead[0] + right[0])

    def resting_columns():
        rows = pl.ds(0, PAD)
        marked = decay[rows] >= 1.0
        start = place[0] * half
        for p in range(2):
            own0 = jnp.zeros((PAD, nx), jnp.float32)
            own1 = jnp.zeros((PAD, nx), jnp.float32)
            for j in range(half):
                f = f_in[2 * j + p, rows]
                own0 = own0 + f
                own1 = own1 + (start + j).astype(jnp.float32) * f
            left0 = sides[p, rows]
            right1 = sides[2 + p, rows]
            all0 = totals[p, rows]
            all1 = totals[2 + p, rows]
            right0 = all0 - own0 - left0
            left1 = all1 - own1 - right1
            prefix = jnp.zeros((PAD, nx), jnp.float32)
            twice = jnp.zeros((PAD, nx), jnp.float32)
            first, last = (0, half + 1) if p == 0 else (-1, half)
            for j in range(first, last):
                t = (start + j).astype(jnp.float32)
                if j > 0:
                    twice = twice + prefix
                if 0 <= j < half:
                    prefix = prefix + f_in[2 * j + p, rows]
                value = 0.5 * (t * (left0 - right0 - own0) + (right1 - left1 + own1)) + twice
                value = value - t * (t * all0 - 2.0 * all1) * (0.5 / period)
                z = 2 * j + p + 1
                hat[z, rows] = jnp.where(marked, value, hat[z, rows])

    def invert(first, count, slot):
        cols = jnp.concatenate([hat[first + i] for i in range(count)], axis=1)
        out = left_product(qy[...], cols)
        out = jnp.concatenate([out[:, i * nx : (i + 1) * nx] for i in range(count)], axis=0)
        out = right_product(out, qx[...])
        for i in range(count):
            phi[slot + i] = out[i * tall : (i + 1) * tall]

    @pl.when(step == 0)
    def _():
        f_copy().start()
        for k in range(steps):
            a_copy(k).start()
        f_copy().wait()

        def body(i, carry):
            sweep(pl.multiple_of(i * SWEEP, SWEEP))
            return carry

        lax.fori_loop(0, ny // SWEEP, body, 0)
        resting_columns()
        invert(0, 2, 0)

    invert(step * chunk + 2, chunk, 2)
    a_copy(step).wait()

    for i in range(chunk):
        at = step * chunk + i
        size = min(TILE, rows_out)
        for y0 in range(0, rows_out, size):
            rows = pl.ds(y0, size)
            layer = i + 1
            here = phi[layer, pl.ds(PAD + y0, size)]
            av[0, at, rows] = av[0, at, rows] - (
                pltpu.roll(here, nx - 1, 1) - pltpu.roll(here, 1, 1)
            )
            av[1, at, rows] = av[1, at, rows] - (
                phi[layer, pl.ds(PAD + y0 + 1, size)] - phi[layer, pl.ds(PAD + y0 - 1, size)]
            )
            av[2, at, rows] = av[2, at, rows] - (
                phi[layer + 1, pl.ds(PAD + y0, size)] - phi[layer - 1, pl.ds(PAD + y0, size)]
            )
    for i in range(2):
        phi[i] = phi[chunk + i]
    v_copy(step).start()

    @pl.when(step + 1 == steps)
    def _():
        for k in range(steps):
            v_copy(k).wait()


def pairs_of(count):
    return [(i, j) for i in range(count) for j in range(i + 1)]


def piece_copies(x_hbm, x_ref, rows, sems):
    return [
        pltpu.make_async_copy(
            x_hbm.at[:, pl.ds(k * rows, rows)], x_ref.at[:, pl.ds(k * rows, rows)], sems.at[k]
        )
        for k in range(x_ref.shape[1] // rows)
    ]


def gram_kernel(count, rows, x_hbm, out_ref, x_ref, acc, sems):
    step = pl.program_id(0)
    copies = piece_copies(x_hbm, x_ref, rows, sems)

    @pl.when(step == 0)
    def _():
        for copy in copies:
            copy.start()
        acc[...] = jnp.zeros(acc.shape, jnp.float32)

    for k, copy in enumerate(copies):
        pl.when(step == k)(copy.wait)

    group = 8
    for bi in range(0, count, group):
        for bj in range(0, bi + 1, group):
            pairs = [
                (i, j)
                for i in range(bi, min(bi + group, count))
                for j in range(bj, min(bj + group, count))
                if j <= i
            ]
            slots = [i * (i + 1) // 2 + j for i, j in pairs]

            def body(t, sums):
                part = pl.ds(pl.multiple_of(step * rows + t * 8, 8), 8)
                needed = sorted({i for i, _ in pairs} | {j for _, j in pairs})
                tile = {i: x_ref[i, part] for i in needed}
                return tuple(s + tile[i] * tile[j] for s, (i, j) in zip(sums, pairs))

            sums = lax.fori_loop(0, rows // 8, body, tuple(acc[s] for s in slots), unroll=4)
            for s, value in zip(slots, sums):
                acc[s] = value

    @pl.when(step == pl.num_programs(0) - 1)
    def _():
        shape = out_ref.shape
        row = lax.broadcasted_iota(jnp.int32, shape, 0)
        lane = lax.broadcasted_iota(jnp.int32, shape, 1)
        out = jnp.zeros(shape, jnp.float32)
        for s, (i, j) in enumerate(pairs_of(count)):
            total = jnp.sum(jnp.sum(acc[s], axis=0, keepdims=True), axis=1, keepdims=True)
            for at in {i * count + j, j * count + i}:
                out = jnp.where((row == at // shape[1]) & (lane == at % shape[1]), total, out)
        out_ref[...] = out


def ortho_kernel(count, rows, cells, parts_ref, x_hbm, out_ref, growth_ref, x_ref, coef, sems):
    step = pl.program_id(0)
    copies = piece_copies(x_hbm, x_ref, rows, sems)

    @pl.when(step == 0)
    def _():
        for copy in copies:
            copy.start()
        nx = x_ref.shape[2]
        shape = (max(8, count), nx)
        row = lax.broadcasted_iota(jnp.int32, shape, 0)
        lane = lax.broadcasted_iota(jnp.int32, shape, 1)
        flat = jnp.sum(parts_ref[...], axis=0) / cells
        work = jnp.where(lane == row + count, 1.0, 0.0)
        for i in range(count):
            at, shift = i * count // nx, i * count % nx
            line = flat[at : at + 1]
            if shift > 0:
                line = pltpu.roll(line, nx - shift, 1)
            work = jnp.where((row == i) & (lane < count), line, work)
        for k in range(count - 1):
            pivot = work[k : k + 1, k : k + 1]
            scale = jnp.where(row[:, :1] > k, work[:, k : k + 1] / pivot, 0.0)
            work = work - scale * work[k : k + 1, :]
        diagonal = jnp.sum(jnp.where(lane == row, work, 0.0), axis=1, keepdims=True)
        across = jnp.sum(jnp.where(lane == row, work, 0.0), axis=0, keepdims=True)
        growth_ref[...] = 0.5 * jnp.log(across[:, :count])
        work = work / jnp.sqrt(diagonal)
        for s, (i, j) in enumerate(pairs_of(count)):
            coef[s] = jnp.broadcast_to(
                work[i : i + 1, count + j : count + j + 1], coef.shape[1:]
            )

    for k, copy in enumerate(copies):
        pl.when(step == k)(copy.wait)

    def body(t, carry):
        part = pl.ds(pl.multiple_of(step * rows + t * 16, 16), 16)
        tile = [x_ref[i, part] for i in range(count)]
        for i in range(count):
            total = None
            for j in range(i + 1):
                c = coef[i * (i + 1) // 2 + j]
                term = jnp.concatenate([c, c], axis=0) * tile[j]
                total = term if total is None else total + term
            out_ref[i, part] = total
        return carry

    lax.fori_loop(0, rows // 16, body, 0, unroll=2)


def params(limit):
    return pltpu.CompilerParams(vmem_limit_bytes=limit * MIB)


def whole(_):
    return pl.BlockSpec(memory_space=pltpu.VMEM)


ANY = pl.BlockSpec(memory_space=pl.ANY)
HBM = pl.BlockSpec(memory_space=pltpu.HBM)
SMEM = pl.BlockSpec(memory_space=pltpu.SMEM)


def rates(place, extra, velocity, halos, tables):
    _, layers, ny, nx = velocity.shape
    tangent = extra.ndim == 4
    chunk = 4 if layers % 4 == 0 else 2
    field = pltpu.VMEM((3, layers + 4, ny + 2 * PAD, nx), jnp.float32)
    scratch = [field, field] if tangent else [field]
    scratch += [
        pltpu.VMEM((3, ny, nx), jnp.float32),
        pltpu.VMEM((ny + 2 * PAD, nx), jnp.float32),
        pltpu.VMEM((chunk, ny, nx), jnp.float32),
        pltpu.VMEM((ny, nx), jnp.float32),
        pltpu.VMEM(velocity.shape, jnp.float32),
        pltpu.VMEM((chunk, ny, nx), jnp.float32),
        pltpu.VMEM((layers, ny, nx), jnp.float32),
        *[pltpu.VMEM(t.shape, t.dtype) for t in tables],
        pltpu.SemaphoreType.DMA((layers // chunk, 2)),
        pltpu.SemaphoreType.DMA((2, 4)),
        pltpu.SemaphoreType.DMA((layers // chunk, 2)),
        pltpu.SemaphoreType.DMA((2,)),
    ]
    size = velocity.size
    return pl.pallas_call(
        functools.partial(rate_kernel, tangent, len(halos) > 0, chunk, layers),
        grid=(layers // chunk,),
        in_specs=[SMEM, ANY if tangent else SMEM, ANY]
        + [ANY for _ in halos]
        + [HBM for _ in tables],
        out_specs=[ANY, ANY, whole((4, ny, nx))],
        out_shape=[
            jax.ShapeDtypeStruct(velocity.shape, jnp.float32),
            jax.ShapeDtypeStruct((layers, ny, nx), jnp.float32),
            jax.ShapeDtypeStruct((4, ny, nx), jnp.float32),
        ],
        scratch_shapes=scratch,
        compiler_params=params(52 if tangent else 28),
        cost_estimate=pl.CostEstimate(
            flops=60 * size, bytes_accessed=16 * size, transcendentals=0
        ),
        name="tangent_rates" if tangent else "base_rates",
    )(place, extra, velocity, *halos, *tables)


def edge_rates(place, tangent, velocity, halos, a, f, moments, tables):
    _, layers, ny, nx = velocity.shape
    field = pltpu.VMEM((3, 12, ny + 2 * PAD, nx), jnp.float32)
    ends = layers // 2 - 1
    return pl.pallas_call(
        functools.partial(edge_kernel, layers),
        grid=(2,),
        in_specs=[SMEM] + [ANY] * 6 + [whole(moments.shape)] + [HBM for _ in tables],
        out_specs=[
            pl.BlockSpec((3, 2, ny, nx), lambda g: (0, g * ends, 0, 0)),
            pl.BlockSpec((2, ny, nx), lambda g: (g * ends, 0, 0)),
            whole((4, ny, nx)),
        ],
        out_shape=[
            jax.ShapeDtypeStruct(a.shape, jnp.float32),
            jax.ShapeDtypeStruct(f.shape, jnp.float32),
            jax.ShapeDtypeStruct(moments.shape, jnp.float32),
        ],
        scratch_shapes=[
            field,
            field,
            pltpu.VMEM((3, ny, nx), jnp.float32),
            pltpu.VMEM((ny + 2 * PAD, nx), jnp.float32),
            pltpu.VMEM((2, ny, nx), jnp.float32),
            *[pltpu.VMEM(t.shape, t.dtype) for t in tables],
            pltpu.SemaphoreType.DMA((2, 2)),
            pltpu.SemaphoreType.DMA((2, 4)),
            pltpu.SemaphoreType.DMA((2,)),
        ],
        input_output_aliases={5: 0, 6: 1},
        compiler_params=params(52),
        cost_estimate=pl.CostEstimate(
            flops=60 * 12 * ny * nx, bytes_accessed=160 * ny * nx, transcendentals=0
        ),
        name="tangent_edges",
    )(place, tangent, velocity, *halos, a, f, moments, *tables)


def solve(place, f, sides, totals, wraps, tables, a, rows_out, period):
    layers, ny, nx = f.shape
    chunk = 8 if layers % 8 == 0 else 2
    tall = rows_out + 2 * PAD
    moments = whole((4, ny, nx))
    return pl.pallas_call(
        functools.partial(solve_kernel, chunk, layers, period, rows_out),
        grid_spec=pltpu.PrefetchScalarGridSpec(
            num_scalar_prefetch=1,
            grid=(layers // chunk,),
            in_specs=[ANY, moments, moments, whole((ny, nx)), whole((ny, nx))]
            + [whole(t.shape) for t in tables]
            + [ANY],
            out_specs=ANY,
            scratch_shapes=[
                pltpu.VMEM((layers, ny, nx), jnp.float32),
                pltpu.VMEM((3, layers, rows_out, nx), jnp.float32),
                pltpu.VMEM((layers, ny, nx), jnp.float32),
                pltpu.VMEM((layers + 2, ny, nx), jnp.float32),
                pltpu.VMEM((chunk + 2, tall, nx), jnp.float32),
                pltpu.SemaphoreType.DMA,
                pltpu.SemaphoreType.DMA((layers // chunk,)),
                pltpu.SemaphoreType.DMA((layers // chunk,)),
            ],
        ),
        out_shape=jax.ShapeDtypeStruct((3, layers, rows_out, nx), jnp.float32),
        compiler_params=params(52 if rows_out == ny else 16),
        cost_estimate=pl.CostEstimate(
            flops=40 * a.size, bytes_accessed=12 * a.size, transcendentals=0
        ),
        name="tangent_solve" if rows_out == ny else "base_solve",
    )(place, f, sides, totals, *wraps, *tables, a)


def row_chunk(rows):
    best = 16
    for size in range(16, 400, 16):
        if rows % size == 0:
            best = size
    return best


def gram(cells):
    count, rows, nx = cells.shape
    size = row_chunk(rows)
    tall = -(-count * count // nx)
    return pl.pallas_call(
        functools.partial(gram_kernel, count, size),
        grid=(rows // size,),
        in_specs=[ANY],
        out_specs=whole((tall, nx)),
        out_shape=jax.ShapeDtypeStruct((tall, nx), jnp.float32),
        scratch_shapes=[
            pltpu.VMEM(cells.shape, jnp.float32),
            pltpu.VMEM((count * (count + 1) // 2, 8, nx), jnp.float32),
            pltpu.SemaphoreType.DMA((rows // size,)),
        ],
        compiler_params=params(14),
        cost_estimate=pl.CostEstimate(
            flops=count * cells.size, bytes_accessed=4 * cells.size, transcendentals=0
        ),
        name="gram_parts",
    )(cells)


def ortho(parts, cells, total_cells):
    count, rows, nx = cells.shape
    size = row_chunk(rows)
    return pl.pallas_call(
        functools.partial(ortho_kernel, count, size, total_cells),
        grid=(rows // size,),
        in_specs=[whole(parts.shape), ANY],
        out_specs=[whole(cells.shape), whole((1, count))],
        out_shape=[
            jax.ShapeDtypeStruct(cells.shape, jnp.float32),
            jax.ShapeDtypeStruct((1, count), jnp.float32),
        ],
        scratch_shapes=[
            pltpu.VMEM(cells.shape, jnp.float32),
            pltpu.VMEM((count * (count + 1) // 2, 8, nx), jnp.float32),
            pltpu.SemaphoreType.DMA((rows // size,)),
        ],
        compiler_params=params(24),
        cost_estimate=pl.CostEstimate(
            flops=count * cells.size, bytes_accessed=8 * cells.size, transcendentals=0
        ),
        name="ortho_rows",
    )(parts, cells)


def ring_shift(block, shift):
    count = lax.axis_size("gz")
    return lax.ppermute(block, "gz", [(i, (i + shift) % count) for i in range(count)])


def side_sums(moments, slab_power):
    count = lax.axis_size("gz")
    here = lax.axis_index("gz")
    right, left = moments[:2], moments[2:]
    from_left = jnp.zeros_like(right)
    from_right = jnp.zeros_like(left)
    span = 1
    while span < count:
        swapped = lax.ppermute(
            jnp.concatenate([right, left], axis=0), "gz", [(i, i ^ span) for i in range(count)]
        )
        other_right, other_left = swapped[:2], swapped[2:]
        inside = here % span
        upper = (here // span) % 2 == 1
        to_left = slab_power(inside)
        to_right = slab_power(span - 1 - inside)
        from_left = jnp.where(upper, from_left + to_left * other_right, from_left)
        from_right = jnp.where(upper, from_right, from_right + to_right * other_left)
        across = slab_power(span)
        right = jnp.where(upper, right + across * other_right, other_right + across * right)
        left = jnp.where(upper, other_left + across * left, left + across * other_left)
        span *= 2
    return jnp.concatenate([from_left, from_right], axis=0), jnp.concatenate([right, left], axis=0)


def per_device(base_flow, tangents, shells):
    _, layers, ny, nx = base_flow.shape
    slabs = lax.axis_size("gz")
    vectors = lax.axis_size("vec")
    here = lax.axis_index("gz")
    mine = lax.axis_index("vec")
    nz = slabs * layers
    period = nz // 2
    tangent = tangents[0]

    basis_x, sines_x = real_basis(nx)
    basis_y, sines_y = real_basis(ny)
    decay64, resting = column_tables(sines_y, sines_x)
    decay = jnp.asarray(decay64, jnp.float32)
    slab_log = jnp.asarray((layers // 2) * np.log(decay64), jnp.float32)
    closing = jnp.asarray(
        np.where(resting, 0.0, 1.0 / np.where(resting, 1.0, 1.0 - decay64**period)), jnp.float32
    )

    def slab_power(exponent):
        return jnp.exp(jnp.asarray(exponent).astype(jnp.float32) * slab_log)

    wraps = (closing * slab_power(here), closing * slab_power(slabs - 1 - here))
    forward = jnp.asarray(np.concatenate([right_table(basis_x), left_table(basis_y.T)], axis=0))
    qx_inverse = jnp.asarray(right_table(basis_x.T))
    rows_out = ny // vectors

    def inverse_tables(first, count):
        high, low = halves(np.concatenate([basis_y, basis_y, basis_y], axis=0))
        both = [qx_inverse]
        for part in (high, low):
            part = lax.dynamic_slice_in_dim(jnp.asarray(part), ny + first - PAD, count + 2 * PAD, 0)
            both.append(jnp.concatenate([part, part], axis=1))
        return (decay, jnp.concatenate(both, axis=0))

    def edge(near, far):
        return jnp.concatenate(
            [base_flow[:, near], tangent[:, near], base_flow[2:, far], tangent[2:, far]], axis=0
        )

    lo = ring_shift(edge(layers - 1, layers - 2), 1)
    hi = ring_shift(edge(0, 1), -1)

    rows_run = max(rows_out, LEAST)
    block = mine * rows_out // rows_run
    place = jnp.stack([here, block]).astype(jnp.int32)
    rate_tables = (decay, forward)
    a, f, moments = rates(place, tangent, base_flow, (), rate_tables)
    a, f, moments = edge_rates(place, tangent, base_flow, (lo, hi), a, f, moments, rate_tables)
    sides, totals = side_sums(moments, slab_power)
    tables = inverse_tables(0, ny)
    advanced = solve(place, f, sides, totals, wraps, tables, a, ny, period)
    advanced, base_lo, base_hi = lax.optimization_barrier((advanced, lo, hi))

    piece_rows = 3 * layers * ny // vectors
    cells = lax.all_to_all(
        advanced.reshape(vectors, piece_rows, nx), "vec", split_axis=0, concat_axis=0, tiled=True
    )

    positions = (here * layers + jnp.arange(layers, dtype=jnp.int32)) % nz
    angles = 2.0 * math.pi / nz * (shells[:, None] * positions[None, :] % nz).astype(jnp.float32)
    profile = time_step * forcing_amplitude * jnp.sum(jnp.sin(angles), axis=0)
    base_a, base_f, base_moments = rates(place, profile, base_flow, (base_lo, base_hi), rate_tables)
    base_sides, base_totals = side_sums(base_moments, slab_power)
    tables = inverse_tables(block * rows_run, rows_run)
    base_rows = solve(
        place, base_f, base_sides, base_totals, wraps, tables, base_a, rows_run, period
    )
    if rows_run != rows_out:
        base_rows = lax.dynamic_slice_in_dim(
            base_rows, mine * rows_out - block * rows_run, rows_out, 2
        )

    cells, base_rows = lax.optimization_barrier((cells, base_rows))
    part = gram(cells)
    devices = slabs * vectors
    if devices <= 64:
        parts = lax.all_to_all(
            jnp.broadcast_to(part[None], (devices,) + part.shape),
            ("vec", "gz"),
            split_axis=0,
            concat_axis=0,
            tiled=True,
        )
    else:
        parts = lax.psum(part, ("vec", "gz"))[None]
    ortho_cells, growth = ortho(parts, cells, 3.0 * nz * ny * nx)
    ortho_cells, growth = lax.optimization_barrier((ortho_cells, growth.reshape(vectors)))
    returned = lax.all_to_all(ortho_cells, "vec", split_axis=0, concat_axis=0, tiled=True)
    return (base_rows, returned.reshape(tangents.shape), growth)


def solution(mesh):
    in_specs = (P(None, "gz", None, None), P("vec", None, "gz", None, None), P())
    out_specs = (P(None, "gz", "vec", None), P("vec", None, "gz", None, None), P())
    return jax.shard_map(
        per_device, mesh=mesh, in_specs=in_specs, out_specs=out_specs, check_vma=False
    )
```

```python
import functools
import math

import jax
import jax.numpy as jnp
import ml_dtypes
import numpy as np
from jax import lax
from jax.experimental import pallas as pl
from jax.experimental.pallas import tpu as pltpu
from jax.sharding import PartitionSpec as P

time_step = 0.005
viscosity = 0.01
forcing_amplitude = 4.0

TILE = 128
SWEEP = 32
LEAST = 16
PAD = 8
MIB = 1024 * 1024


def spacing_of(nx):
    return 2.0 * math.pi / nx


def real_basis(length):
    cells = np.arange(length)
    columns = [np.full(length, 1.0 / np.sqrt(length)), (-1.0) ** cells / np.sqrt(length)]
    waves = [0, length // 2]
    for wave in range(1, length // 2):
        angle = 2.0 * np.pi * ((cells * wave) % length) / length
        columns += [np.sqrt(2.0 / length) * np.cos(angle), np.sqrt(2.0 / length) * np.sin(angle)]
        waves += [wave, wave]
    sines = np.sin(2.0 * np.pi * np.array(waves) / length) ** 2
    sines[:2] = 0.0
    return np.stack(columns, axis=1), sines


def halves(matrix):
    high = matrix.astype(np.float32).astype(ml_dtypes.bfloat16)
    low = (matrix - high.astype(np.float64)).astype(np.float32).astype(ml_dtypes.bfloat16)
    return high, low


def right_table(matrix):
    high, low = halves(matrix)
    return np.concatenate(
        [np.concatenate([high, low], axis=1), np.concatenate([high, low], axis=1)], axis=0
    )


def left_table(matrix):
    high, low = halves(matrix)
    return np.concatenate(
        [np.concatenate([high, high], axis=1), np.concatenate([low, low], axis=1)], axis=0
    )


def column_tables(sines_y, sines_x):
    four = 4.0 * (sines_y[:, None] + sines_x[None, :])
    resting = four == 0.0
    decay = 1.0 / (1.0 + four / 2.0 + np.sqrt(four + four * four / 4.0))
    return decay, resting


def split_cat(data, axis):
    high = data.astype(jnp.bfloat16)
    low = (data - high.astype(jnp.float32)).astype(jnp.bfloat16)
    return jnp.concatenate([high, low], axis=axis)


def right_product(data, table):
    out = jnp.dot(split_cat(data, 1), table, preferred_element_type=jnp.float32)
    width = out.shape[1] // 2
    return out[:, :width] + out[:, width:]


def left_product(table, data):
    out = jnp.dot(table, split_cat(data, 0), preferred_element_type=jnp.float32)
    height = out.shape[0] // 2
    return out[:height] + out[height:]


def power_of(base, exponent):
    out = None
    while exponent > 0:
        if exponent % 2 == 1:
            out = base if out is None else out * base
        base = base * base
        exponent //= 2
    return out


def wrap_rows(ref, index, ny):
    ref[index + (pl.ds(0, PAD),)] = ref[index + (pl.ds(ny, PAD),)]
    ref[index + (pl.ds(ny + PAD, PAD),)] = ref[index + (pl.ds(PAD, PAD),)]


def halo_pairs(source, fields, near, far, inner, sems, side):
    out = []
    for i, (_, ref) in enumerate(fields):
        out += [
            pltpu.make_async_copy(
                source.at[pl.ds(3 * i, 3)], ref.at[:, near, inner], sems.at[side, 2 * i]
            ),
            pltpu.make_async_copy(source.at[6 + i], ref.at[2, far, inner], sems.at[side, 2 * i + 1]),
        ]
    return out


def rate_tile(us, vs, layer, y0, comps):
    nx = vs.shape[3]
    space = spacing_of(nx)
    adv_scale = -time_step / (2.0 * space)
    lap_scale = viscosity * time_step / (space * space)
    rows = pl.ds(PAD + y0, TILE)
    flow = [vs[c, layer, rows] for c in range(3)]
    drift = flow if us is None else [us[c, layer, rows] for c in range(3)]
    out = []

    def neighbours(ref, c, centre):
        return (
            pltpu.roll(centre, nx - 1, 1),
            pltpu.roll(centre, 1, 1),
            ref[c, layer, pl.ds(PAD + y0 + 1, TILE)],
            ref[c, layer, pl.ds(PAD + y0 - 1, TILE)],
            ref[c, layer + 1, rows],
            ref[c, layer - 1, rows],
        )

    for c in comps:
        xp, xm, yp, ym, zp, zm = neighbours(vs if us is None else us, c, drift[c])
        adv = flow[0] * (xp - xm) + flow[1] * (yp - ym) + flow[2] * (zp - zm)
        lap = ((xp + xm) + (yp + ym)) + ((zp + zm) - 6.0 * drift[c])
        if us is not None:
            xp, xm, yp, ym, zp, zm = neighbours(vs, c, flow[c])
            adv = adv + (drift[0] * (xp - xm) + drift[1] * (yp - ym) + drift[2] * (zp - zm))
        out.append(adv_scale * adv + lap_scale * lap)
    return drift, out


def z_rate(fns, layer, slot):
    us, vs, rz = fns[:3]
    for y0 in range(0, rz.shape[1], TILE):
        _, (rate,) = rate_tile(us, vs, layer, y0, (2,))
        rz[slot, pl.ds(y0, TILE)] = rate


def layer_rates(fns, layer, i, slot, shift):
    us, vs, rz, ry, dv, a_out = fns
    ny, nx = rz.shape[1:]
    for y0 in range(0, ny, TILE):
        rows = pl.ds(y0, TILE)
        drift, (rate_x, rate_y) = rate_tile(us, vs, layer, y0, (0, 1))
        if shift is not None:
            rate_x = rate_x + shift
        a_out[0, slot, rows] = drift[0] + rate_x
        a_out[1, slot, rows] = drift[1] + rate_y
        a_out[2, slot, rows] = drift[2] + rz[1, rows]
        dv[i, rows] = pltpu.roll(rate_x, nx - 1, 1) - pltpu.roll(rate_x, 1, 1)
        ry[pl.ds(PAD + y0, TILE)] = rate_y
    z_rate(fns, layer + 1, 2)
    wrap_rows(ry, (), ny)
    for y0 in range(0, ny, TILE):
        rows = pl.ds(y0, TILE)
        along_y = ry[pl.ds(PAD + y0 + 1, TILE)] - ry[pl.ds(PAD + y0 - 1, TILE)]
        middle, upper = rz[1, rows], rz[2, rows]
        along_z = upper - rz[0, rows]
        dv[i, rows] = dv[i, rows] + (along_y + along_z)
        rz[0, rows] = middle
        rz[1, rows] = upper


def transform(dv, f_out, basis, chunk):
    ny, nx = dv.shape[1:]
    qx, qy = basis.at[pl.ds(0, 2 * nx)], basis.at[pl.ds(2 * nx, 2 * ny)]
    waves = right_product(dv[...].reshape(chunk * ny, nx), qx[...]).reshape(chunk, ny, nx)
    waves = left_product(qy[...], jnp.concatenate([waves[i] for i in range(chunk)], axis=1))
    for i in range(chunk):
        f_out[i] = waves[:, i * nx : (i + 1) * nx]


def rate_kernel(tangent, halos, chunk, layers, *refs):
    if tangent:
        (place, u_hbm, v_hbm), refs = refs[:3], refs[3:]
    else:
        (place, profile, v_hbm), refs = refs[:3], refs[3:]
    if halos:
        (lo_hbm, hi_hbm), refs = refs[:2], refs[2:]
    (decay_hbm, basis_hbm, a_hbm, f_hbm, m_out), refs = refs[:5], refs[5:]
    if tangent:
        us, refs = refs[0], refs[1:]
    (vs, rz, ry, dv, pw, a_out, f_out, f_all, decay, basis) = refs[:10]
    (sems, halo_sems, out_sems, table_sems) = refs[10:]
    if not tangent:
        us = vs
    step = pl.program_id(0)
    steps = layers // chunk
    ny = f_out.shape[1]
    fields = [(v_hbm, vs)]
    if tangent:
        fields.append((u_hbm, us))
    inner = pl.ds(PAD, ny)

    def chunk_copies(k):
        return [
            pltpu.make_async_copy(
                source.at[:, pl.ds(k * chunk, chunk)],
                target.at[:, pl.ds(k * chunk + 2, chunk), inner],
                sems.at[k, i],
            )
            for i, (source, target) in enumerate(fields)
        ]

    def halo_copies(side):
        source = (lo_hbm, hi_hbm)[side]
        near, far = ((1, 0), (layers + 2, layers + 3))[side]
        return halo_pairs(source, fields, near, far, inner, halo_sems, side)

    def table_copies():
        return [
            pltpu.make_async_copy(decay_hbm, decay, table_sems.at[0]),
            pltpu.make_async_copy(basis_hbm, basis, table_sems.at[1]),
        ]

    def out_copies(k):
        part = pl.ds(k * chunk, chunk)
        return [
            pltpu.make_async_copy(a_out.at[:, part], a_hbm.at[:, part], out_sems.at[k, 0]),
            pltpu.make_async_copy(f_all.at[part], f_hbm.at[part], out_sems.at[k, 1]),
        ]

    def wait_chunk(k):
        for copy in chunk_copies(k):
            copy.wait()

        def body(i, carry):
            for _, ref in fields:
                for c in range(3):
                    wrap_rows(ref, (c, k * chunk + 2 + i), ny)
            return carry

        lax.fori_loop(0, chunk, body, 0)

    def wait_halo(side):
        for copy in halo_copies(side):
            copy.wait()
        near, far = ((1, 0), (layers + 2, layers + 3))[side]
        for _, ref in fields:
            for c in range(3):
                wrap_rows(ref, (c, near), ny)
            wrap_rows(ref, (2, far), ny)

    fns = (us if tangent else None, vs, rz, ry, dv, a_out)

    @pl.when(step == 0)
    def _():
        if halos:
            for copy in halo_copies(0):
                copy.start()
        for k in range(steps):
            for copy in chunk_copies(k):
                copy.start()
            if k == 0:
                for copy in table_copies():
                    copy.start()
        if halos:
            for copy in halo_copies(1):
                copy.start()
            wait_halo(0)
        wait_chunk(0)
        if halos:
            if steps == 1:
                wait_halo(1)
            z_rate(fns, 1, 0)
            z_rate(fns, 2, 1)
        for copy in table_copies():
            copy.wait()
        m_out[...] = jnp.zeros(m_out.shape, jnp.float32)
        start = (place[0] * (layers // 2)).astype(jnp.float32)
        pw[...] = jnp.where(decay[...] >= 1.0, start, 1.0)

    @pl.when(step + 1 < steps)
    def _():
        wait_chunk(step + 1)

    if halos and steps > 1:

        @pl.when(step + 1 == steps)
        def _():
            wait_halo(1)

    for i in range(chunk):
        shift = None if tangent else profile[step * chunk + i]
        layer_rates(fns, step * chunk + i + 2, i, step * chunk + i, shift)
    transform(dv, f_out, basis, chunk)
    for i in range(chunk):
        f_all[step * chunk + i] = f_out[i]
    for copy in out_copies(step):
        copy.start()

    for y0 in range(0, ny, TILE):
        rows = pl.ds(y0, TILE)
        rate = decay[rows]
        marks = jnp.where(rate >= 1.0, 1.0, 0.0)
        power = pw[rows]
        right = [m_out[0, rows], m_out[1, rows]]
        left = [m_out[2, rows], m_out[3, rows]]
        for i in range(chunk):
            parity = i % 2
            f = f_out[i, rows]
            ahead = rate * right[parity] + f
            if not halos:
                if i < 2:
                    f = jnp.where(step > 0, f, 0.0)
                    ahead = rate * right[parity] + f
                if i >= chunk - 2:
                    f = jnp.where(step + 1 < steps, f, 0.0)
                    ahead = jnp.where(step + 1 < steps, ahead, right[parity])
            right[parity] = ahead
            left[parity] = left[parity] + power * f
            if parity == 1:
                power = rate * power + marks
        pw[rows] = power
        m_out[0, rows], m_out[1, rows] = right
        m_out[2, rows], m_out[3, rows] = left

    @pl.when(step + 1 == steps)
    def _():
        for k in range(steps):
            for copy in out_copies(k):
                copy.wait()


def edge_kernel(layers, *refs):
    (place, u_hbm, v_hbm, lo_hbm, hi_hbm, a_in, f_in, m_in, decay_hbm, basis_hbm) = refs[:10]
    (a_out, f_out, m_out, us, vs, rz, ry, dv, decay, basis) = refs[10:20]
    (sems, halo_sems, table_sems) = refs[20:]
    step = pl.program_id(0)
    ny = f_out.shape[1]
    fields = [(v_hbm, vs), (u_hbm, us)]
    inner = pl.ds(PAD, ny)

    def copies(side):
        source = (lo_hbm, hi_hbm)[side]
        near, far = ((1, 0), (10, 11))[side]
        first, slot = ((0, 2), (layers - 4, 6))[side]
        return halo_pairs(source, fields, near, far, inner, halo_sems, side) + [
            pltpu.make_async_copy(
                ref.at[:, pl.ds(first, 4)], target.at[:, pl.ds(slot, 4), inner], sems.at[side, i]
            )
            for i, (ref, target) in enumerate(fields)
        ]

    def arrive(side):
        for copy in copies(side):
            copy.wait()
        near, far = ((1, 0), (10, 11))[side]
        for _, ref in fields:
            for layer in range(6 * side, 6 * side + 6):
                for c in range(3):
                    if layer != far or c == 2:
                        wrap_rows(ref, (c, layer), ny)

    tables = [
        pltpu.make_async_copy(decay_hbm, decay, table_sems.at[0]),
        pltpu.make_async_copy(basis_hbm, basis, table_sems.at[1]),
    ]

    @pl.when(step == 0)
    def _():
        for copy in copies(0) + tables + copies(1):
            copy.start()
        arrive(0)
        for copy in tables:
            copy.wait()

    @pl.when(step == 1)
    def _():
        arrive(1)

    fns = (us, vs, rz, ry, dv, a_out)
    top = step * 6 + 2
    z_rate(fns, top - 1, 0)
    z_rate(fns, top, 1)
    for i in range(2):
        layer_rates(fns, top + i, i, i, None)
    transform(dv, f_out, basis, 2)
    half = layers // 2
    start = place[0] * half
    last = power_of(decay[...], half - 1)

    @pl.when(step == 0)
    def _():
        weight = jnp.where(decay[...] >= 1.0, start.astype(jnp.float32), 1.0)
        for p in range(2):
            m_out[p] = decay[...] * m_in[p] + last * f_out[p]
            m_out[2 + p] = m_in[2 + p] + weight * f_out[p]

    @pl.when(step == 1)
    def _():
        weight = jnp.where(decay[...] >= 1.0, (start + half - 1).astype(jnp.float32), last)
        for p in range(2):
            m_out[p] = m_out[p] + f_out[p]
            m_out[2 + p] = m_out[2 + p] + weight * f_out[p]


def solve_kernel(chunk, layers, period, rows_out, *refs):
    (place, f_hbm, sides, totals, wrap_l, wrap_r, decay, basis, a_hbm) = refs[:9]
    (v_hbm, f_in, av, qm, hat, phi, f_sem, a_sems, v_sems) = refs[9:]
    step = pl.program_id(0)
    steps = layers // chunk
    ny, nx = f_in.shape[1], f_in.shape[2]
    tall = rows_out + 2 * PAD
    half = layers // 2
    qx, qy = basis.at[pl.ds(0, 2 * nx)], basis.at[pl.ds(2 * nx, 2 * tall)]

    def f_copy():
        return pltpu.make_async_copy(f_hbm, f_in, f_sem)

    def a_copy(k):
        part = pl.ds(k * chunk, chunk)
        rows = pl.ds(0, rows_out)
        if rows_out < ny:
            rows = pl.ds(pl.multiple_of(place[1] * rows_out, rows_out), rows_out)
        return pltpu.make_async_copy(a_hbm.at[:, part, rows], av.at[:, part], a_sems.at[k])

    def v_copy(k):
        part = pl.ds(k * chunk, chunk)
        return pltpu.make_async_copy(av.at[:, part], v_hbm.at[:, part], v_sems.at[k])

    def sweep(y0):
        rows = pl.ds(y0, SWEEP)
        rate = decay[rows]
        resting = rate >= 1.0
        factor = jnp.where(resting, 0.0, -rate / jnp.where(resting, 1.0, 1.0 - rate * rate))
        left = [sides[p, rows] + wrap_l[rows] * totals[p, rows] for p in range(2)]
        right = [sides[2 + p, rows] + wrap_r[rows] * totals[2 + p, rows] for p in range(2)]
        back = list(right)
        for z in reversed(range(layers)):
            f = f_in[z, rows]
            part = rate * back[z % 2]
            qm[z, rows] = part
            back[z % 2] = part + f
        hat[0, rows] = factor * (left[1] + rate * back[1])
        ahead = list(left)
        for z in range(layers):
            ahead[z % 2] = rate * ahead[z % 2] + f_in[z, rows]
            hat[z + 1, rows] = factor * (ahead[z % 2] + qm[z, rows])
        hat[layers + 1, rows] = factor * (rate * ahead[0] + right[0])

    def resting_columns():
        rows = pl.ds(0, PAD)
        marked = decay[rows] >= 1.0
        start = place[0] * half
        for p in range(2):
            own0 = jnp.zeros((PAD, nx), jnp.float32)
            own1 = jnp.zeros((PAD, nx), jnp.float32)
            for j in range(half):
                f = f_in[2 * j + p, rows]
                own0 = own0 + f
                own1 = own1 + (start + j).astype(jnp.float32) * f
            left0 = sides[p, rows]
            right1 = sides[2 + p, rows]
            all0 = totals[p, rows]
            all1 = totals[2 + p, rows]
            right0 = all0 - own0 - left0
            left1 = all1 - own1 - right1
            prefix = jnp.zeros((PAD, nx), jnp.float32)
            twice = jnp.zeros((PAD, nx), jnp.float32)
            first, last = (0, half + 1) if p == 0 else (-1, half)
            for j in range(first, last):
                t = (start + j).astype(jnp.float32)
                if j > 0:
                    twice = twice + prefix
                if 0 <= j < half:
                    prefix = prefix + f_in[2 * j + p, rows]
                value = 0.5 * (t * (left0 - right0 - own0) + (right1 - left1 + own1)) + twice
                value = value - t * (t * all0 - 2.0 * all1) * (0.5 / period)
                z = 2 * j + p + 1
                hat[z, rows] = jnp.where(marked, value, hat[z, rows])

    def invert(first, count, slot):
        cols = jnp.concatenate([hat[first + i] for i in range(count)], axis=1)
        out = left_product(qy[...], cols)
        out = jnp.concatenate([out[:, i * nx : (i + 1) * nx] for i in range(count)], axis=0)
        out = right_product(out, qx[...])
        for i in range(count):
            phi[slot + i] = out[i * tall : (i + 1) * tall]

    @pl.when(step == 0)
    def _():
        f_copy().start()
        for k in range(steps):
            a_copy(k).start()
        f_copy().wait()

        def body(i, carry):
            sweep(pl.multiple_of(i * SWEEP, SWEEP))
            return carry

        lax.fori_loop(0, ny // SWEEP, body, 0)
        resting_columns()
        invert(0, 2, 0)

    invert(step * chunk + 2, chunk, 2)
    a_copy(step).wait()

    for i in range(chunk):
        at = step * chunk + i
        size = min(TILE, rows_out)
        for y0 in range(0, rows_out, size):
            rows = pl.ds(y0, size)
            layer = i + 1
            here = phi[layer, pl.ds(PAD + y0, size)]
            av[0, at, rows] = av[0, at, rows] - (
                pltpu.roll(here, nx - 1, 1) - pltpu.roll(here, 1, 1)
            )
            av[1, at, rows] = av[1, at, rows] - (
                phi[layer, pl.ds(PAD + y0 + 1, size)] - phi[layer, pl.ds(PAD + y0 - 1, size)]
            )
            av[2, at, rows] = av[2, at, rows] - (
                phi[layer + 1, pl.ds(PAD + y0, size)] - phi[layer - 1, pl.ds(PAD + y0, size)]
            )
    for i in range(2):
        phi[i] = phi[chunk + i]
    v_copy(step).start()

    @pl.when(step + 1 == steps)
    def _():
        for k in range(steps):
            v_copy(k).wait()


def pairs_of(count):
    return [(i, j) for i in range(count) for j in range(i + 1)]


def piece_copies(x_hbm, x_ref, rows, sems):
    return [
        pltpu.make_async_copy(
            x_hbm.at[:, pl.ds(k * rows, rows)], x_ref.at[:, pl.ds(k * rows, rows)], sems.at[k]
        )
        for k in range(x_ref.shape[1] // rows)
    ]


def gram_kernel(count, rows, x_hbm, out_ref, x_ref, acc, sems):
    step = pl.program_id(0)
    copies = piece_copies(x_hbm, x_ref, rows, sems)

    @pl.when(step == 0)
    def _():
        for copy in copies:
            copy.start()
        acc[...] = jnp.zeros(acc.shape, jnp.float32)

    for k, copy in enumerate(copies):
        pl.when(step == k)(copy.wait)

    group = 8
    for bi in range(0, count, group):
        for bj in range(0, bi + 1, group):
            pairs = [
                (i, j)
                for i in range(bi, min(bi + group, count))
                for j in range(bj, min(bj + group, count))
                if j <= i
            ]
            slots = [i * (i + 1) // 2 + j for i, j in pairs]

            def body(t, sums):
                part = pl.ds(pl.multiple_of(step * rows + t * 8, 8), 8)
                needed = sorted({i for i, _ in pairs} | {j for _, j in pairs})
                tile = {i: x_ref[i, part] for i in needed}
                return tuple(s + tile[i] * tile[j] for s, (i, j) in zip(sums, pairs))

            sums = lax.fori_loop(0, rows // 8, body, tuple(acc[s] for s in slots), unroll=4)
            for s, value in zip(slots, sums):
                acc[s] = value

    @pl.when(step == pl.num_programs(0) - 1)
    def _():
        shape = out_ref.shape
        row = lax.broadcasted_iota(jnp.int32, shape, 0)
        lane = lax.broadcasted_iota(jnp.int32, shape, 1)
        out = jnp.zeros(shape, jnp.float32)
        for s, (i, j) in enumerate(pairs_of(count)):
            total = jnp.sum(jnp.sum(acc[s], axis=0, keepdims=True), axis=1, keepdims=True)
            for at in {i * count + j, j * count + i}:
                out = jnp.where((row == at // shape[1]) & (lane == at % shape[1]), total, out)
        out_ref[...] = out


def ortho_kernel(count, rows, cells, parts_ref, x_hbm, out_ref, growth_ref, x_ref, coef, sems):
    step = pl.program_id(0)
    copies = piece_copies(x_hbm, x_ref, rows, sems)

    @pl.when(step == 0)
    def _():
        for copy in copies:
            copy.start()
        nx = x_ref.shape[2]
        shape = (max(8, count), nx)
        row = lax.broadcasted_iota(jnp.int32, shape, 0)
        lane = lax.broadcasted_iota(jnp.int32, shape, 1)
        flat = jnp.sum(parts_ref[...], axis=0) / cells
        work = jnp.where(lane == row + count, 1.0, 0.0)
        for i in range(count):
            at, shift = i * count // nx, i * count % nx
            line = flat[at : at + 1]
            if shift > 0:
                line = pltpu.roll(line, nx - shift, 1)
            work = jnp.where((row == i) & (lane < count), line, work)
        for k in range(count - 1):
            pivot = work[k : k + 1, k : k + 1]
            scale = jnp.where(row[:, :1] > k, work[:, k : k + 1] / pivot, 0.0)
            work = work - scale * work[k : k + 1, :]
        diagonal = jnp.sum(jnp.where(lane == row, work, 0.0), axis=1, keepdims=True)
        across = jnp.sum(jnp.where(lane == row, work, 0.0), axis=0, keepdims=True)
        growth_ref[...] = 0.5 * jnp.log(across[:, :count])
        work = work / jnp.sqrt(diagonal)
        for s, (i, j) in enumerate(pairs_of(count)):
            coef[s] = jnp.broadcast_to(
                work[i : i + 1, count + j : count + j + 1], coef.shape[1:]
            )

    for k, copy in enumerate(copies):
        pl.when(step == k)(copy.wait)

    def body(t, carry):
        part = pl.ds(pl.multiple_of(step * rows + t * 16, 16), 16)
        tile = [x_ref[i, part] for i in range(count)]
        for i in range(count):
            total = None
            for j in range(i + 1):
                c = coef[i * (i + 1) // 2 + j]
                term = jnp.concatenate([c, c], axis=0) * tile[j]
                total = term if total is None else total + term
            out_ref[i, part] = total
        return carry

    lax.fori_loop(0, rows // 16, body, 0, unroll=2)


def params(limit):
    return pltpu.CompilerParams(vmem_limit_bytes=limit * MIB)


def whole(_):
    return pl.BlockSpec(memory_space=pltpu.VMEM)


ANY = pl.BlockSpec(memory_space=pl.ANY)
HBM = pl.BlockSpec(memory_space=pltpu.HBM)
SMEM = pl.BlockSpec(memory_space=pltpu.SMEM)


def rates(place, extra, velocity, halos, tables):
    _, layers, ny, nx = velocity.shape
    tangent = extra.ndim == 4
    chunk = 4 if layers % 4 == 0 else 2
    field = pltpu.VMEM((3, layers + 4, ny + 2 * PAD, nx), jnp.float32)
    scratch = [field, field] if tangent else [field]
    scratch += [
        pltpu.VMEM((3, ny, nx), jnp.float32),
        pltpu.VMEM((ny + 2 * PAD, nx), jnp.float32),
        pltpu.VMEM((chunk, ny, nx), jnp.float32),
        pltpu.VMEM((ny, nx), jnp.float32),
        pltpu.VMEM(velocity.shape, jnp.float32),
        pltpu.VMEM((chunk, ny, nx), jnp.float32),
        pltpu.VMEM((layers, ny, nx), jnp.float32),
        *[pltpu.VMEM(t.shape, t.dtype) for t in tables],
        pltpu.SemaphoreType.DMA((layers // chunk, 2)),
        pltpu.SemaphoreType.DMA((2, 4)),
        pltpu.SemaphoreType.DMA((layers // chunk, 2)),
        pltpu.SemaphoreType.DMA((2,)),
    ]
    size = velocity.size
    return pl.pallas_call(
        functools.partial(rate_kernel, tangent, len(halos) > 0, chunk, layers),
        grid=(layers // chunk,),
        in_specs=[SMEM, ANY if tangent else SMEM, ANY]
        + [ANY for _ in halos]
        + [HBM for _ in tables],
        out_specs=[ANY, ANY, whole((4, ny, nx))],
        out_shape=[
            jax.ShapeDtypeStruct(velocity.shape, jnp.float32),
            jax.ShapeDtypeStruct((layers, ny, nx), jnp.float32),
            jax.ShapeDtypeStruct((4, ny, nx), jnp.float32),
        ],
        scratch_shapes=scratch,
        compiler_params=params(52 if tangent else 28),
        cost_estimate=pl.CostEstimate(
            flops=60 * size, bytes_accessed=16 * size, transcendentals=0
        ),
        name="tangent_rates" if tangent else "base_rates",
    )(place, extra, velocity, *halos, *tables)


def edge_rates(place, tangent, velocity, halos, a, f, moments, tables):
    _, layers, ny, nx = velocity.shape
    field = pltpu.VMEM((3, 12, ny + 2 * PAD, nx), jnp.float32)
    ends = layers // 2 - 1
    return pl.pallas_call(
        functools.partial(edge_kernel, layers),
        grid=(2,),
        in_specs=[SMEM] + [ANY] * 6 + [whole(moments.shape)] + [HBM for _ in tables],
        out_specs=[
            pl.BlockSpec((3, 2, ny, nx), lambda g: (0, g * ends, 0, 0)),
            pl.BlockSpec((2, ny, nx), lambda g: (g * ends, 0, 0)),
            whole((4, ny, nx)),
        ],
        out_shape=[
            jax.ShapeDtypeStruct(a.shape, jnp.float32),
            jax.ShapeDtypeStruct(f.shape, jnp.float32),
            jax.ShapeDtypeStruct(moments.shape, jnp.float32),
        ],
        scratch_shapes=[
            field,
            field,
            pltpu.VMEM((3, ny, nx), jnp.float32),
            pltpu.VMEM((ny + 2 * PAD, nx), jnp.float32),
            pltpu.VMEM((2, ny, nx), jnp.float32),
            *[pltpu.VMEM(t.shape, t.dtype) for t in tables],
            pltpu.SemaphoreType.DMA((2, 2)),
            pltpu.SemaphoreType.DMA((2, 4)),
            pltpu.SemaphoreType.DMA((2,)),
        ],
        input_output_aliases={5: 0, 6: 1},
        compiler_params=params(52),
        cost_estimate=pl.CostEstimate(
            flops=60 * 12 * ny * nx, bytes_accessed=160 * ny * nx, transcendentals=0
        ),
        name="tangent_edges",
    )(place, tangent, velocity, *halos, a, f, moments, *tables)


def solve(place, f, sides, totals, wraps, tables, a, rows_out, period):
    layers, ny, nx = f.shape
    chunk = next(size for size in (16, 8, 2) if layers % size == 0)
    tall = rows_out + 2 * PAD
    moments = whole((4, ny, nx))
    return pl.pallas_call(
        functools.partial(solve_kernel, chunk, layers, period, rows_out),
        grid_spec=pltpu.PrefetchScalarGridSpec(
            num_scalar_prefetch=1,
            grid=(layers // chunk,),
            in_specs=[ANY, moments, moments, whole((ny, nx)), whole((ny, nx))]
            + [whole(t.shape) for t in tables]
            + [ANY],
            out_specs=ANY,
            scratch_shapes=[
                pltpu.VMEM((layers, ny, nx), jnp.float32),
                pltpu.VMEM((3, layers, rows_out, nx), jnp.float32),
                pltpu.VMEM((layers, ny, nx), jnp.float32),
                pltpu.VMEM((layers + 2, ny, nx), jnp.float32),
                pltpu.VMEM((chunk + 2, tall, nx), jnp.float32),
                pltpu.SemaphoreType.DMA,
                pltpu.SemaphoreType.DMA((layers // chunk,)),
                pltpu.SemaphoreType.DMA((layers // chunk,)),
            ],
        ),
        out_shape=jax.ShapeDtypeStruct((3, layers, rows_out, nx), jnp.float32),
        compiler_params=params(52 if rows_out == ny else 16),
        cost_estimate=pl.CostEstimate(
            flops=40 * a.size, bytes_accessed=12 * a.size, transcendentals=0
        ),
        name="tangent_solve" if rows_out == ny else "base_solve",
    )(place, f, sides, totals, *wraps, *tables, a)


def row_chunk(rows):
    best = 16
    for size in range(16, 400, 16):
        if rows % size == 0:
            best = size
    return best


def gram(cells):
    count, rows, nx = cells.shape
    size = row_chunk(rows)
    tall = -(-count * count // nx)
    return pl.pallas_call(
        functools.partial(gram_kernel, count, size),
        grid=(rows // size,),
        in_specs=[ANY],
        out_specs=whole((tall, nx)),
        out_shape=jax.ShapeDtypeStruct((tall, nx), jnp.float32),
        scratch_shapes=[
            pltpu.VMEM(cells.shape, jnp.float32),
            pltpu.VMEM((count * (count + 1) // 2, 8, nx), jnp.float32),
            pltpu.SemaphoreType.DMA((rows // size,)),
        ],
        compiler_params=params(14),
        cost_estimate=pl.CostEstimate(
            flops=count * cells.size, bytes_accessed=4 * cells.size, transcendentals=0
        ),
        name="gram_parts",
    )(cells)


def ortho(parts, cells, total_cells):
    count, rows, nx = cells.shape
    size = row_chunk(rows)
    return pl.pallas_call(
        functools.partial(ortho_kernel, count, size, total_cells),
        grid=(rows // size,),
        in_specs=[whole(parts.shape), ANY],
        out_specs=[whole(cells.shape), whole((1, count))],
        out_shape=[
            jax.ShapeDtypeStruct(cells.shape, jnp.float32),
            jax.ShapeDtypeStruct((1, count), jnp.float32),
        ],
        scratch_shapes=[
            pltpu.VMEM(cells.shape, jnp.float32),
            pltpu.VMEM((count * (count + 1) // 2, 8, nx), jnp.float32),
            pltpu.SemaphoreType.DMA((rows // size,)),
        ],
        compiler_params=params(24),
        cost_estimate=pl.CostEstimate(
            flops=count * cells.size, bytes_accessed=8 * cells.size, transcendentals=0
        ),
        name="ortho_rows",
    )(parts, cells)


def ring_shift(block, shift):
    count = lax.axis_size("gz")
    return lax.ppermute(block, "gz", [(i, (i + shift) % count) for i in range(count)])


def side_sums(moments, slab_power):
    count = lax.axis_size("gz")
    here = lax.axis_index("gz")
    right, left = moments[:2], moments[2:]
    from_left = jnp.zeros_like(right)
    from_right = jnp.zeros_like(left)
    span = 1
    while span < count:
        swapped = lax.ppermute(
            jnp.concatenate([right, left], axis=0), "gz", [(i, i ^ span) for i in range(count)]
        )
        other_right, other_left = swapped[:2], swapped[2:]
        inside = here % span
        upper = (here // span) % 2 == 1
        to_left = slab_power(inside)
        to_right = slab_power(span - 1 - inside)
        from_left = jnp.where(upper, from_left + to_left * other_right, from_left)
        from_right = jnp.where(upper, from_right, from_right + to_right * other_left)
        across = slab_power(span)
        right = jnp.where(upper, right + across * other_right, other_right + across * right)
        left = jnp.where(upper, other_left + across * left, left + across * other_left)
        span *= 2
    return jnp.concatenate([from_left, from_right], axis=0), jnp.concatenate([right, left], axis=0)


def per_device(base_flow, tangents, shells):
    _, layers, ny, nx = base_flow.shape
    slabs = lax.axis_size("gz")
    vectors = lax.axis_size("vec")
    here = lax.axis_index("gz")
    mine = lax.axis_index("vec")
    nz = slabs * layers
    period = nz // 2
    tangent = tangents[0]

    basis_x, sines_x = real_basis(nx)
    basis_y, sines_y = real_basis(ny)
    decay64, resting = column_tables(sines_y, sines_x)
    decay = jnp.asarray(decay64, jnp.float32)
    slab_log = jnp.asarray((layers // 2) * np.log(decay64), jnp.float32)
    closing = jnp.asarray(
        np.where(resting, 0.0, 1.0 / np.where(resting, 1.0, 1.0 - decay64**period)), jnp.float32
    )

    def slab_power(exponent):
        return jnp.exp(jnp.asarray(exponent).astype(jnp.float32) * slab_log)

    wraps = (closing * slab_power(here), closing * slab_power(slabs - 1 - here))
    forward = jnp.asarray(np.concatenate([right_table(basis_x), left_table(basis_y.T)], axis=0))
    qx_inverse = jnp.asarray(right_table(basis_x.T))
    rows_out = ny // vectors

    def inverse_tables(first, count):
        high, low = halves(np.concatenate([basis_y, basis_y, basis_y], axis=0))
        both = [qx_inverse]
        for part in (high, low):
            part = lax.dynamic_slice_in_dim(jnp.asarray(part), ny + first - PAD, count + 2 * PAD, 0)
            both.append(jnp.concatenate([part, part], axis=1))
        return (decay, jnp.concatenate(both, axis=0))

    def edge(near, far):
        return jnp.concatenate(
            [base_flow[:, near], tangent[:, near], base_flow[2:, far], tangent[2:, far]], axis=0
        )

    lo = ring_shift(edge(layers - 1, layers - 2), 1)
    hi = ring_shift(edge(0, 1), -1)

    rows_run = max(rows_out, LEAST)
    block = mine * rows_out // rows_run
    place = jnp.stack([here, block]).astype(jnp.int32)
    rate_tables = (decay, forward)
    a, f, moments = rates(place, tangent, base_flow, (), rate_tables)
    a, f, moments = edge_rates(place, tangent, base_flow, (lo, hi), a, f, moments, rate_tables)
    sides, totals = side_sums(moments, slab_power)
    tables = inverse_tables(0, ny)
    advanced = solve(place, f, sides, totals, wraps, tables, a, ny, period)
    advanced, base_lo, base_hi = lax.optimization_barrier((advanced, lo, hi))

    piece_rows = 3 * layers * ny // vectors
    cells = lax.all_to_all(
        advanced.reshape(vectors, piece_rows, nx), "vec", split_axis=0, concat_axis=0, tiled=True
    )

    positions = (here * layers + jnp.arange(layers, dtype=jnp.int32)) % nz
    angles = 2.0 * math.pi / nz * (shells[:, None] * positions[None, :] % nz).astype(jnp.float32)
    profile = time_step * forcing_amplitude * jnp.sum(jnp.sin(angles), axis=0)
    base_a, base_f, base_moments = rates(place, profile, base_flow, (base_lo, base_hi), rate_tables)
    base_sides, base_totals = side_sums(base_moments, slab_power)
    tables = inverse_tables(block * rows_run, rows_run)
    base_rows = solve(
        place, base_f, base_sides, base_totals, wraps, tables, base_a, rows_run, period
    )
    if rows_run != rows_out:
        base_rows = lax.dynamic_slice_in_dim(
            base_rows, mine * rows_out - block * rows_run, rows_out, 2
        )

    cells, base_rows = lax.optimization_barrier((cells, base_rows))
    part = gram(cells)
    devices = slabs * vectors
    if devices <= 64:
        parts = lax.all_to_all(
            jnp.broadcast_to(part[None], (devices,) + part.shape),
            ("vec", "gz"),
            split_axis=0,
            concat_axis=0,
            tiled=True,
        )
    else:
        parts = lax.psum(part, ("vec", "gz"))[None]
    ortho_cells, growth = ortho(parts, cells, 3.0 * nz * ny * nx)
    ortho_cells, growth = lax.optimization_barrier((ortho_cells, growth.reshape(vectors)))
    returned = lax.all_to_all(ortho_cells, "vec", split_axis=0, concat_axis=0, tiled=True)
    return (base_rows, returned.reshape(tangents.shape), growth)


def solution(mesh):
    in_specs = (P(None, "gz", None, None), P("vec", None, "gz", None, None), P())
    out_specs = (P(None, "gz", "vec", None), P("vec", None, "gz", None, None), P())
    return jax.shard_map(
        per_device, mesh=mesh, in_specs=in_specs, out_specs=out_specs, check_vma=False
    )
```
